128 devices in a mesh: rep: 32 (over y_lo, x, z), tp: 4 (over y_hi, core).
Axes of the slice: x: 4, y: 4 (y_hi: 2, y_lo: 2; y = y_hi * 2 + y_lo), z: 4, core: 2. Of those that a mesh axis runs over, the one named last changes fastest.
Arguments:
- tokens: bfloat16 [14336, 5120], P('rep', 'tp'), may hold values from -6 to 6
- prompt_rows: bfloat16 [4096, 5120], P('rep', 'tp'), may hold values from -6 to 6
- norm_gain: float32 [5120], replicated, may hold values from 0.5 to 2
- w_query: float32 [5120, 4096], P(('rep', 'tp')), may hold values from -0.078125 to 0.078125
- w_key: float32 [5120, 512], P(('rep', 'tp')), may hold values from -0.078125 to 0.078125
- w_value: float32 [5120, 512], P(('rep', 'tp')), may hold values from -0.078125 to 0.078125
- w_out: float32 [4096, 5120], P(None, ('rep', 'tp')), may hold values from -0.09375 to 0.09375
- q_gain: float32 [128], replicated, may hold values from 0.5 to 2.5
- k_gain: float32 [128], replicated, may hold values from 0.5 to 2.5
- seq_lengths: int32 [4], replicated, may hold values from 1 to 224, 448 in all
- prompt_group: int32 [128], P('rep'), may hold values from 0 to 31
- prompt_blocks: int32 [128], P('rep'), may hold values from 1 to 2
- dest_offset: int32 [4], replicated, may hold values from 0 to 31
Outputs:
- returned: bfloat16 [14336, 5120], P('rep', 'tp')
The draws below stay inside these ranges and needn't reach their ends.
Inputs may be any that keep to these rules, and one draw needn't show every extreme that they name: `seq_lengths`: the same lengths hold on every replica and sum to 448. Slot j of replica s returns to learner shard (s + dest_offset[j]) mod 32, at the same rows.
All inputs are finite; a program needn't handle non-finite values.
Results may differ from the reference program's by a relative error of at most 0.013.
Values may be sent and summed in bfloat16 or wider, within the bound.
A program may use at most 128 MiB of HBM per device.

```python
import math
import jax
import jax.numpy as jnp
import numpy as np
from jax import lax

D = 5120
HD = 128
TOK_DEV = 448
SEQ_DEV = 4
PTOK_DEV = 128
PBLOCKS = 2
PBLK = 64
MAXLEN = 224
QW = 4096
KW = 512
TOKENS = 14336
SEQS = 128
PTOKENS = 4096
N_REP = 32


def touch_ends(result, rng, low, largest):
    place = [jax.random.randint(jax.random.fold_in(rng, axis), (), 0, length) for axis, length in enumerate(result.shape)]
    longest = result.shape.index(max(result.shape))
    beside = place[:longest] + [(place[longest] + 1) % result.shape[longest]] + place[longest + 1:]
    return result.at[tuple(place)].set(low).at[tuple(beside)].set(largest)


def levels(rng, shape, shards, smallest, high):
    loudness = 1.0
    for axis_at, blocks in shards:
        heights = jax.random.uniform(jax.random.fold_in(jax.random.fold_in(rng, 6), axis_at), (blocks,), jnp.float32, smallest / len(shards), high / len(shards))
        loudness = loudness * jnp.repeat(jnp.exp(heights), shape[axis_at] // blocks).reshape((-1,) + (1,) * (len(shape) - 1 - axis_at))
    return loudness


def split_up(count, total, most, slope):
    loads = [(1 << 20) // math.isqrt(standing ** slope) + 1 for standing in range(2, count + 1)]
    surplus, holding = total - most - (count - 1), [1] * (count - 1)
    while surplus > 0:
        free = [i for i in range(count - 1) if holding[i] < most]
        mass, left = sum([loads[i] for i in free]), surplus
        for i in free:
            addition = min(most - holding[i], max(1, left * loads[i] // mass), surplus)
            holding[i] = holding[i] + addition
            surplus = surplus - addition
    return np.array([most] + holding)


def ragged_sizes(rng, count, total, most, skew):
    if count == 2:
        one = jax.random.randint(rng, (), max(1, total - most), min(most, total - 1) + 1)
        return jnp.stack([one, total - one])
    sizes = jnp.asarray(split_up(count, total, most, skew), jnp.int32)
    couples = (count - 1) // 2
    source_of, sink = sizes[1:1 + 2 * couples:2], sizes[2:2 + 2 * couples:2]
    slack = jnp.minimum(source_of - 1, most - sink)
    shifted = jax.random.randint(jax.random.fold_in(rng, 1), (couples,), 0, 1 << 20) % (slack + 1)
    sizes = sizes.at[1:1 + 2 * couples:2].set(source_of - shifted).at[2:2 + 2 * couples:2].set(sink + shifted)
    return sizes[jax.random.permutation(jax.random.fold_in(rng, 2), count)]


def normal_values(stream_key, shape, deviation, limit, pieces=(), held_as=jnp.bfloat16):
    array = deviation * jax.random.normal(stream_key, shape, jnp.float32)
    if pieces:
        array = array * levels(stream_key, shape, pieces, -0.22, 0.18)
    return jnp.clip(array, -limit, limit).astype(held_as)


def setup_inputs(seed: int = 0) -> dict:
    arg_keys = jax.random.split(jax.random.key(seed), 14)
    tokens = normal_values(arg_keys[0], (TOKENS, D), 1.0, 6.0, ((0, 32), (1, 4)))
    prompt_rows = normal_values(arg_keys[1], (PTOKENS, D), 1.0, 6.0, ((0, 32), (1, 4)))
    norm_gain = jnp.clip(jnp.exp(jax.random.uniform(arg_keys[2], (D,), jnp.float32, math.log(0.5), math.log(2.0))), 0.5, 2.0)
    w_query = normal_values(arg_keys[3], (D, QW), D ** -0.5, 0.078125, ((0, 128),), jnp.float32)
    w_key = normal_values(arg_keys[4], (D, KW), D ** -0.5, 0.078125, ((0, 128),), jnp.float32)
    w_value = normal_values(arg_keys[5], (D, KW), D ** -0.5, 0.078125, ((0, 128),), jnp.float32)
    w_out = normal_values(arg_keys[6], (QW, D), QW ** -0.5, 0.09375, ((1, 128),), jnp.float32)
    q_gain = jnp.clip(jnp.exp(jax.random.uniform(arg_keys[7], (HD,), jnp.float32, math.log(0.5), math.log(2.5))), 0.5, 2.5)
    k_gain = jnp.clip(jnp.exp(jax.random.uniform(arg_keys[8], (HD,), jnp.float32, math.log(0.5), math.log(2.5))), 0.5, 2.5)
    seq_lengths = ragged_sizes(arg_keys[9], SEQ_DEV, TOK_DEV, MAXLEN, 2).astype(jnp.int32)
    prompt_group = touch_ends(jax.random.randint(arg_keys[10], (SEQS,), 0, N_REP), jax.random.fold_in(arg_keys[10], 1), 0, N_REP - 1).astype(jnp.int32)
    prompt_blocks = touch_ends(jax.random.randint(arg_keys[11], (SEQS,), 1, PBLOCKS + 1), jax.random.fold_in(arg_keys[11], 1), 1, PBLOCKS).astype(jnp.int32)
    dest_offset = touch_ends(jax.random.randint(arg_keys[12], (SEQ_DEV,), 0, N_REP), jax.random.fold_in(arg_keys[12], 1), 0, N_REP - 1).astype(jnp.int32)
    return dict(tokens=tokens, prompt_rows=prompt_rows, norm_gain=norm_gain, w_query=w_query, w_key=w_key, w_value=w_value, w_out=w_out, q_gain=q_gain, k_gain=k_gain, seq_lengths=seq_lengths, prompt_group=prompt_group, prompt_blocks=prompt_blocks, dest_offset=dest_offset)


epsilon = 1e-06
rope_base = 1000000.0

def rms_rows(values, gain_row):
    floats = values.astype(jnp.float32)
    scaled = lax.rsqrt(lax.optimization_barrier(jnp.mean(floats * floats, axis=-1, keepdims=True)) + epsilon)
    return floats * scaled * gain_row

def rotary(values, positions):
    half_size = values.shape[-1] // 2
    spread = jnp.arange(half_size, dtype=jnp.float32) * (2.0 / values.shape[-1])
    frequency = rope_base ** (-spread)
    angles = positions.astype(jnp.float32)[:, None] * frequency[None, :]
    cosine = jnp.cos(angles)[:, None, :]
    sine_part = jnp.sin(angles)[:, None, :]
    front_half = values[..., :half_size]
    back_half = values[..., half_size:]
    return jnp.concatenate([front_half * cosine - back_half * sine_part, back_half * cosine + front_half * sine_part], axis=-1)

def slot_layout(seq_lengths, row_count):
    ends_at = jnp.cumsum(seq_lengths).astype(jnp.int32)
    starts_at = ends_at - seq_lengths
    position = jnp.arange(row_count, dtype=jnp.int32)
    slot_of = lax.optimization_barrier(jnp.sum((position[:, None] >= ends_at[None, :]).astype(jnp.int32), axis=1))
    onehot = (slot_of[:, None] == jnp.arange(seq_lengths.shape[0], dtype=jnp.int32)[None, :]).astype(jnp.int32)
    within = position - lax.optimization_barrier(jnp.sum(onehot * starts_at[None, :], axis=1))
    return (slot_of, within, onehot)

def attend(queries, own_keys, own_values, shared_keys, shared_values, slot_of, prefix_len, prompt_len):
    row_count = queries.shape[0]
    head_size = queries.shape[-1]
    all_keys = jnp.concatenate([shared_keys, own_keys], axis=0).astype(jnp.float32)
    all_values = jnp.concatenate([shared_values, own_values], axis=0).astype(jnp.float32)
    shared_index = jnp.arange(shared_keys.shape[0], dtype=jnp.int32)
    shared_mask = ((shared_index // prompt_len)[None, :] == slot_of[:, None]) & ((shared_index % prompt_len)[None, :] < prefix_len[:, None])
    position = jnp.arange(row_count, dtype=jnp.int32)
    own_mask = (slot_of[None, :] == slot_of[:, None]) & (position[None, :] <= position[:, None])
    allowed = jnp.concatenate([shared_mask, own_mask], axis=1)
    scores = jnp.einsum('rkgd,nkd->kgrn', queries.astype(jnp.float32), all_keys) * head_size ** (-0.5)
    weights = jnp.where(allowed[None, None], jnp.exp(scores), 0.0)
    weighted = (weights / lax.optimization_barrier(jnp.sum(weights, axis=-1, keepdims=True))).astype(jnp.bfloat16)
    blended = jnp.einsum('kgrn,nkd->rkgd', weighted.astype(jnp.float32), all_values)
    return blended.reshape(row_count, -1).astype(jnp.bfloat16)

def reference(tokens, prompt_rows, norm_gain, w_query, w_key, w_value, w_out, q_gain, k_gain, seq_lengths, prompt_group, prompt_blocks, dest_offset):
    query_weight = w_query.astype(jnp.bfloat16)
    key_weight = w_key.astype(jnp.bfloat16)
    value_weight = w_value.astype(jnp.bfloat16)
    out_weight = w_out.astype(jnp.bfloat16)
    head_count = QW // HD
    kv_heads = KW // HD
    group_size = head_count // kv_heads
    normed = rms_rows(tokens, norm_gain).astype(jnp.bfloat16)
    prompt_normed = rms_rows(prompt_rows, norm_gain).astype(jnp.bfloat16)
    prompt_key = jnp.dot(prompt_normed, key_weight, preferred_element_type=jnp.float32).reshape(PTOKENS, kv_heads, HD)
    prompt_pos = jnp.tile(jnp.arange(PTOK_DEV, dtype=jnp.int32), N_REP)
    prompt_key = rotary(rms_rows(prompt_key, k_gain), prompt_pos).astype(jnp.bfloat16).reshape(N_REP, PTOK_DEV, kv_heads, HD)
    prompt_value = jnp.dot(prompt_normed, value_weight, preferred_element_type=jnp.float32).astype(jnp.bfloat16).reshape(N_REP, PTOK_DEV, kv_heads, HD)
    slot_of, within, onehot = slot_layout(seq_lengths, TOK_DEV)

    def one_replica(items):
        replica_rows, groups_here, blocks_here = items
        prefix_len = lax.optimization_barrier(jnp.sum(onehot * (blocks_here * PBLK)[None, :], axis=1))
        positions = prefix_len + within
        queries = jnp.dot(replica_rows, query_weight, preferred_element_type=jnp.float32).reshape(TOK_DEV, head_count, HD)
        queries = rotary(rms_rows(queries, q_gain), positions).astype(jnp.bfloat16).reshape(TOK_DEV, kv_heads, group_size, HD)
        own_keys = jnp.dot(replica_rows, key_weight, preferred_element_type=jnp.float32).reshape(TOK_DEV, kv_heads, HD)
        own_keys = rotary(rms_rows(own_keys, k_gain), positions).astype(jnp.bfloat16)
        own_values = jnp.dot(replica_rows, value_weight, preferred_element_type=jnp.float32).astype(jnp.bfloat16).reshape(TOK_DEV, kv_heads, HD)
        shared_keys = prompt_key[groups_here].reshape(SEQ_DEV * PTOK_DEV, kv_heads, HD)
        shared_values = prompt_value[groups_here].reshape(SEQ_DEV * PTOK_DEV, kv_heads, HD)
        return attend(queries, own_keys, own_values, shared_keys, shared_values, slot_of, prefix_len, PTOK_DEV)
    heads = lax.map(one_replica, (normed.reshape(N_REP, TOK_DEV, D), prompt_group.reshape(N_REP, SEQ_DEV), prompt_blocks.reshape(N_REP, SEQ_DEV)))
    heads = heads.reshape(TOKENS, QW)
    layer = (tokens.astype(jnp.float32) + jnp.dot(heads, out_weight, preferred_element_type=jnp.float32)).astype(jnp.bfloat16)
    layer = layer.reshape(N_REP, TOK_DEV, D)
    shift_rows = lax.optimization_barrier(jnp.sum(onehot * dest_offset[None, :], axis=1))
    source = jnp.mod(jnp.arange(N_REP, dtype=jnp.int32)[:, None] - shift_rows[None, :], N_REP)
    returned = layer[source, jnp.arange(TOK_DEV, dtype=jnp.int32)[None, :]]
    return returned.reshape(TOKENS, D)
```

```python
import functools

import jax
import jax.numpy as jnp
from jax import lax
from jax.experimental import pallas as pl
from jax.experimental.pallas import tpu as pltpu
from jax.sharding import PartitionSpec as P

PBLK = 64
MESH = pl.DeviceIdType.MESH
ANY = pl.BlockSpec(memory_space=pl.ANY)
VMEM = pl.BlockSpec(memory_space=pltpu.VMEM)
OFFSETS = (0, -1, 1, 2)
META = 16

epsilon = 1e-06
rope_base = 1000000.0


def place():
    rep, tp = lax.axis_index("rep"), lax.axis_index("tp")
    return lax.rem(rep // 4, 4), (tp // 2) * 2 + rep // 16, lax.rem(rep, 4), lax.rem(tp, 2)


def device_at(x, y, z, core):
    return (lax.rem(y, 2) * 16 + x * 4 + z, (y // 2) * 2 + core)


def step(value, by):
    return lax.rem(value + (by + 4), 4)


def greet(peers):
    barrier = pltpu.get_barrier_semaphore()
    for peer in peers:
        pl.semaphore_signal(barrier, inc=1, device_id=peer, device_id_type=MESH)
    pl.semaphore_wait(barrier, len(peers))


def send(source, target, send_sem, recv_sem, device):
    return pltpu.make_async_remote_copy(
        src_ref=source,
        dst_ref=target,
        send_sem=send_sem,
        recv_sem=recv_sem,
        device_id=device,
        device_id_type=MESH,
    )


class Plane:
    COPIES = 72

    def __init__(self, view, send_sems, recv_sems):
        self.view, self.ss, self.rs = view, send_sems, recv_sems
        self.x, self.y, self.z, self.core = place()
        self.started = []

    def block(self, half, first, second, part=None):
        a, b = (first, second) if half == 0 else (second, first)
        return self.view(half, step(self.x, a) * 4 + step(self.z, b), part)

    def toward(self, half, phase, sign):
        if (phase == 0) == (half == 0):
            return device_at(step(self.x, sign), self.y, self.z, self.core)
        return device_at(self.x, self.y, step(self.z, sign), self.core)

    def copy(self, half, number, ref, device):
        at = half * 36 + number
        return send(ref, ref, self.ss.at[at], self.rs.at[at], device)

    def start(self, *args):
        made = self.copy(*args)
        made.start()
        self.started.append(made)

    def sibling(self):
        return device_at(self.x, self.y, self.z, 1 - self.core)

    def share(self, half, o1, o2):
        ref = self.block(half, OFFSETS[o1], OFFSETS[o2])
        self.start(half, 20 + 4 * o1 + o2, ref, self.sibling())

    def spread(self, half, o1):
        ref = self.block(half, OFFSETS[o1], 0)
        self.start(half, 4 + 4 * o1, ref, self.toward(half, 1, 1))
        self.start(half, 5 + 4 * o1, ref, self.toward(half, 1, -1))
        self.share(half, o1, 0)

    def begin(self):
        for half in range(2):
            ref = self.block(half, 0, 0)
            self.start(half, 0, ref, self.toward(half, 0, 1))
            self.start(half, 1, ref, self.toward(half, 0, -1))
        for half in range(2):
            self.spread(half, 0)

    def arrived(self, half, number, ref):
        self.copy(half, number, ref, self.sibling()).wait_recv()

    def first(self):
        for half in range(2):
            self.arrived(half, 0, self.block(half, -1, 0))
            self.start(half, 2, self.block(half, -1, 0, 0), self.toward(half, 0, 1))
            self.arrived(half, 1, self.block(half, 1, 0))
            self.start(half, 3, self.block(half, 1, 0, 1), self.toward(half, 0, -1))
        for half in range(2):
            self.spread(half, 1)
            self.spread(half, 2)

    def opposite(self):
        for half in range(2):
            self.arrived(half, 2, self.block(half, 2, 0, 0))
            self.arrived(half, 3, self.block(half, 2, 0, 1))
            self.spread(half, 3)

    def second(self, o1):
        off, base = OFFSETS[o1], 4 + 4 * o1
        for half in range(2):
            self.arrived(half, base, self.block(half, off, -1))
            self.start(half, base + 2, self.block(half, off, -1, 0), self.toward(half, 1, 1))
            self.arrived(half, base + 1, self.block(half, off, 1))
            self.start(half, base + 3, self.block(half, off, 1, 1), self.toward(half, 1, -1))
            self.share(half, o1, 1)
            self.share(half, o1, 2)

    def second_opposite(self, o1):
        off, base = OFFSETS[o1], 4 + 4 * o1
        for half in range(2):
            self.arrived(half, base + 2, self.block(half, off, 2, 0))
            self.arrived(half, base + 3, self.block(half, off, 2, 1))
            self.share(half, o1, 3)

    def second_all(self):
        self.second(0)
        for o1 in range(1, 4):
            self.second(o1)
            self.second_opposite(o1 - 1)
        self.second_opposite(3)

    def finish(self, shared_block):
        for half in range(2):
            for o1 in range(4):
                for o2 in range(4):
                    a, b = (o1, o2) if half == 0 else (o2, o1)
                    where = step(self.x, OFFSETS[a]) * 4 + step(self.z, OFFSETS[b])
                    self.arrived(half, 20 + 4 * o1 + o2, shared_block(half, where))
        for made in self.started:
            made.wait_send()


def gather_kernel(
    x_ref, win_ref, wout_ref, rows_ref, gin_ref, gout_ref,
    a_send, a_recv, in_send, in_recv, out_send, out_recv, t_send, t_recv, local_sem,
):
    x, y, z, core = place()
    rep, tp = lax.axis_index("rep"), lax.axis_index("tp")
    y_lo, y_hi, plane_at = lax.rem(y, 2), y // 2, x * 4 + z
    sibling = device_at(x, y, z, 1 - core)
    column = [(dy, dc) for dy in range(4) for dc in range(2) if (dy, dc) != (0, 0)]

    def other(dy, dc):
        return step(y, dy), (core if dc == 0 else 1 - core)

    peers = [device_at(x, other(dy, dc)[0], z, other(dy, dc)[1]) for dy, dc in column]
    peers += [device_at(step(x, s), y, z, core) for s in (1, -1)]
    peers += [device_at(x, y, step(z, s), core) for s in (1, -1)]
    greet(peers)

    columns = []
    locals_ = []
    for which, (source, target) in enumerate(((win_ref, gin_ref), (wout_ref, gout_ref))):
        made = pltpu.make_async_copy(
            source.at[y * 2 + core], target.at[core, y_lo, plane_at, tp], local_sem.at[which]
        )
        made.start()
        locals_.append(made)
        sent = []
        for n, (dy, dc) in enumerate(column):
            to_y, to_core = other(dy, dc)
            made = send(
                source.at[to_y * 2 + to_core],
                target.at[to_core, y_lo, plane_at, tp],
                a_send.at[which * 7 + n],
                a_recv.at[which * 7 + n],
                device_at(x, to_y, z, to_core),
            )
            made.start()
            sent.append(made)
        columns.append(sent)

    count, width = x_ref.shape
    cut = count // 32 * 16

    def quarter(at):
        return pl.ds(pl.multiple_of(at * width, 128), width)

    def token_copy(number, source, target, device):
        return send(source, target, t_send.at[number], t_recv.at[number], device)

    home = core == y_lo
    mine = rows_ref.at[:, quarter(tp)]
    up = send(x_ref, mine, t_send.at[0], t_recv.at[core], device_at(x, step(y, 1), z, y_lo))
    down = send(x_ref, mine, t_send.at[1], t_recv.at[2 + core], device_at(x, step(y, -1), z, y_lo))
    up.start()
    down.start()

    @pl.when(home)
    def _():
        pltpu.make_async_copy(x_ref, mine, local_sem.at[2]).start()

    @pl.when(jnp.logical_not(home))
    def _():
        token_copy(4, x_ref, mine, sibling).start()

    def ready(which):
        target = (gin_ref, gout_ref)[which]
        locals_[which].wait()
        for n, (dy, dc) in enumerate(column):
            from_y = step(y, -dy)
            from_core = core if dc == 0 else 1 - core
            ref = target.at[core, lax.rem(from_y, 2), plane_at, (from_y // 2) * 2 + from_core]
            send(ref, ref, a_send.at[which * 7 + n], a_recv.at[which * 7 + n], sibling).wait_recv()

    def viewer(target, owner):
        def view(half, where, part=None):
            if part is None:
                return target.at[owner, half, where]
            return target.at[owner, half, where, pl.ds(part * 2, 2)]

        return view

    inward = Plane(viewer(gin_ref, core), in_send, in_recv)
    outward = Plane(viewer(gout_ref, core), out_send, out_recv)
    ready(0)
    inward.begin()
    inward.first()
    inward.opposite()
    ready(1)
    outward.begin()

    def away_blocks():
        below, above = step(y, -1), step(y, 1)
        for k in range(2):
            low = (below // 2) * 2 + k
            high = (above // 2) * 2 + k
            yield k, low, high, below, above

    @pl.when(jnp.logical_not(home))
    def _():
        for k, low, high, below, above in away_blocks():
            ref = rows_ref.at[:, quarter(low)]
            token_copy(k, ref, ref, sibling).wait_recv()
            ref = rows_ref.at[pl.ds(0, cut), quarter(low)]
            token_copy(5 + k, ref, ref, device_at(x, above, z, core)).start()
            ref = rows_ref.at[:, quarter(high)]
            token_copy(2 + k, ref, ref, sibling).wait_recv()
            ref = rows_ref.at[pl.ds(cut, count - cut), quarter(high)]
            token_copy(7 + k, ref, ref, device_at(x, below, z, core)).start()

    inward.second_all()
    outward.first()
    outward.opposite()
    outward.second_all()

    @pl.when(jnp.logical_not(home))
    def _():
        for k, low, high, below, above in away_blocks():
            ref = rows_ref.at[pl.ds(0, cut), quarter(low)]
            token_copy(5 + k, ref, ref, sibling).wait_send()
            ref = rows_ref.at[pl.ds(cut, count - cut), quarter(high)]
            token_copy(7 + k, ref, ref, sibling).wait_send()
        token_copy(4, x_ref, mine, sibling).wait_send()

    @pl.when(home)
    def _():
        opposite = 1 - y_hi
        for k in range(2):
            at = quarter(opposite * 2 + k)
            ref = rows_ref.at[pl.ds(0, cut), at]
            token_copy(5 + k, ref, ref, sibling).wait_recv()
            ref = rows_ref.at[pl.ds(cut, count - cut), at]
            token_copy(7 + k, ref, ref, sibling).wait_recv()
        ref = rows_ref.at[:, quarter(y_hi * 2 + 1 - core)]
        token_copy(4, ref, ref, sibling).wait_recv()
        pltpu.make_async_copy(x_ref, mine, local_sem.at[2]).wait()

    up.wait_send()
    down.wait_send()
    for sent in columns:
        for made in sent:
            made.wait_send()
    inward.finish(viewer(gin_ref, 1 - core))
    outward.finish(viewer(gout_ref, 1 - core))


def gather_all(rows, win, wout):
    count, width = rows.shape
    sems = [14, 14, Plane.COPIES, Plane.COPIES, Plane.COPIES, Plane.COPIES, 9, 9, 3]
    return pl.pallas_call(
        gather_kernel,
        name="gather_all",
        out_shape=(
            jax.ShapeDtypeStruct((count, 4 * width), rows.dtype),
            jax.ShapeDtypeStruct((2, 2, 16, 4) + win.shape[1:], win.dtype),
            jax.ShapeDtypeStruct((2, 2, 16, 4) + wout.shape[1:], wout.dtype),
        ),
        in_specs=[ANY] * 3,
        out_specs=(ANY,) * 3,
        scratch_shapes=[pltpu.SemaphoreType.DMA((n,)) for n in sems],
        compiler_params=pltpu.CompilerParams(collective_id=0, has_side_effects=True),
    )(rows, win, wout)


def prompt_kernel(own_ref, all_ref, send_sems, recv_sems, local_sem):
    x, y, z, core = place()
    peers = [device_at(x, y, z, 1 - core)]
    peers += [device_at(step(x, s), y, z, core) for s in (1, -1)]
    peers += [device_at(x, y, step(z, s), core) for s in (1, -1)]
    greet(peers)
    made = pltpu.make_async_copy(own_ref, all_ref.at[core, x * 4 + z], local_sem.at[0])
    made.start()
    made.wait()

    def viewer(owner):
        def view(half, where, part=None):
            rows = pl.ds(half * 64, 64) if part is None else pl.ds(half * 64 + part * 32, 32)
            return all_ref.at[owner, where, rows]

        return view

    plane = Plane(viewer(core), send_sems, recv_sems)
    plane.begin()
    plane.first()
    plane.opposite()
    plane.second_all()
    plane.finish(viewer(1 - core))


def gather_prompts(own):
    sems = [Plane.COPIES, Plane.COPIES, 1]
    return pl.pallas_call(
        prompt_kernel,
        name="gather_prompts",
        out_shape=jax.ShapeDtypeStruct((2, 16) + own.shape, own.dtype),
        in_specs=[ANY],
        out_specs=ANY,
        scratch_shapes=[pltpu.SemaphoreType.DMA((n,)) for n in sems],
        compiler_params=pltpu.CompilerParams(collective_id=1, has_side_effects=True),
    )(own)


CHUNKS = 4
ORDERS = (
    ("z1", "x2", "y1", "z2", "x1"),
    ("x1", "z2", "x2", "y1", "z1"),
    ("y1", "z1", "x1", "x2", "z2"),
    ("z2", "y1", "z1", "x1", "x2"),
)
SIGNS = (1, -1, 1, -1)


def level_bits(shift, sign):
    odd = shift % 2 == 1
    far = (shift >= 2) if sign == 1 else ((shift == 1) | (shift == 2))
    return odd, far


def move_masks(shift_rows, rep):
    z, x = rep % 4, rep // 4 % 4
    rows = shift_rows.shape[0] // CHUNKS
    masks = []
    for chunk in range(CHUNKS):
        sign = SIGNS[chunk]
        shift = shift_rows[chunk * rows : (chunk + 1) * rows]
        shift_z = shift % 4
        odd_z, far_z = level_bits(shift_z, sign)
        for at, level in enumerate(ORDERS[chunk]):
            later = ORDERS[chunk][at + 1 :]
            end_z = z
            if "z1" in later:
                end_z = end_z + sign * odd_z.astype(jnp.int32)
            if "z2" in later:
                end_z = end_z + 2 * far_z.astype(jnp.int32)
            end_z = (end_z + 4) % 4
            carry_z = (end_z < shift_z).astype(jnp.int32)
            need_x = shift // 4 % 4 + carry_z
            shift_x = need_x % 4
            odd_x, far_x = level_bits(shift_x, sign)
            end_x = x
            if "x1" in later:
                end_x = end_x + sign * odd_x.astype(jnp.int32)
            if "x2" in later:
                end_x = end_x + 2 * far_x.astype(jnp.int32)
            end_x = (end_x + 4) % 4
            carry_x = (end_x < need_x).astype(jnp.int32)
            shift_y = (shift // 16 + carry_x) % 2
            masks.append(
                {"z1": odd_z, "z2": far_z, "x1": odd_x, "x2": far_x, "y1": shift_y == 1}[level]
            )
    masks = jnp.stack(masks).astype(jnp.float32)
    return jnp.broadcast_to(
        masks.reshape(CHUNKS, len(ORDERS[0]), rows, 1), (CHUNKS, len(ORDERS[0]), rows, 128)
    )


def return_kernel(
    part_ref, tokens_ref, mask_ref, out_ref,
    raw, final, summed, held, landed,
    raw_send, raw_recv, fin_send, fin_recv, sib_send, sib_recv, move_send, move_recv,
):
    x, y, z, core = place()
    y_lo, y_hi = lax.rem(y, 2), y // 2
    width = tokens_ref.shape[1]
    rows = tokens_ref.shape[0] // CHUNKS
    above, below = step(y, 1), step(y, -1)
    sibling = device_at(x, y, z, 1 - core)
    peers = [device_at(x, at, z, k) for at in (above, below) for k in range(2)] + [sibling]
    peers += [device_at(step(x, s), y, z, core) for s in (1, -1, 2)]
    peers += [device_at(x, y, step(z, s), core) for s in (1, -1, 2)]
    greet(peers)
    home = core == y_lo

    def block(chunk):
        return pl.ds(chunk * rows, rows)

    def part(chunk, quarter):
        return part_ref.at[block(chunk), pl.ds(pl.multiple_of(quarter * width, 128), width)]

    def raw_copy(chunk, slot):
        quarter = (1 - y_hi) * 2 + slot
        to = device_at(x, (above, below)[slot], z, core)
        at = slot * CHUNKS + chunk
        return send(part(chunk, quarter), raw.at[slot, block(chunk)], raw_send.at[at], raw_recv.at[at], to)

    def sibling_copy(chunk):
        return send(
            part(chunk, y_hi * 2 + 1 - core), final.at[2, block(chunk)],
            sib_send.at[chunk], sib_recv.at[chunk], sibling,
        )

    def final_copy(chunk, slot, k):
        to_y = (above, below)[slot]
        if slot == k:
            source = summed.at[slot, block(chunk)]
        else:
            source = part(chunk, (to_y // 2) * 2 + k)
        at = slot * CHUNKS + chunk
        return send(
            source, final.at[slot, block(chunk)],
            fin_send.at[at + k * 2 * CHUNKS], fin_recv.at[at], device_at(x, to_y, z, k),
        )

    @pl.when(home)
    def _():
        for chunk in range(CHUNKS):
            raw_copy(chunk, 0).start()
            raw_copy(chunk, 1).start()
            sibling_copy(chunk).start()

    @pl.when(jnp.logical_not(home))
    def _():
        for chunk in range(CHUNKS):
            for slot in range(2):
                final_copy(chunk, slot, 1 - slot).start()
        for chunk in range(CHUNKS):
            for slot in range(2):
                raw_copy(chunk, slot).wait_recv()
                quarter = ((above, below)[slot] // 2) * 2 + slot
                summed[slot, block(chunk)] = (
                    part(chunk, quarter)[...].astype(jnp.float32)
                    + raw[slot, block(chunk)].astype(jnp.float32)
                ).astype(jnp.bfloat16)
                final_copy(chunk, slot, slot).start()

    def target(level, sign):
        by = sign if level[1] == "1" else 2
        if level[0] == "z":
            return device_at(x, y, step(z, by), core)
        if level[0] == "x":
            return device_at(step(x, by), y, z, core)
        return device_at(x, y_hi * 2 + 1 - y_lo, z, core)

    def move(chunk, at):
        number = at * CHUNKS + chunk
        return send(
            held.at[at, block(chunk)], landed.at[at, block(chunk)],
            move_send.at[number], move_recv.at[number], target(ORDERS[chunk][at], SIGNS[chunk]),
        )

    steps = len(ORDERS[0])
    for chunk in range(CHUNKS):
        for slot in range(2):
            final_copy(chunk, slot, 0).wait_recv()

        @pl.when(home)
        def _():
            final[2, block(chunk)] = part(chunk, y_hi * 2 + core)[...]

        @pl.when(jnp.logical_not(home))
        def _():
            sibling_copy(chunk).wait_recv()

        total = final[0, block(chunk)].astype(jnp.float32) + final[1, block(chunk)].astype(jnp.float32)
        total = total + final[2, block(chunk)].astype(jnp.float32)
        held[0, block(chunk)] = (
            tokens_ref[block(chunk)].astype(jnp.float32) + total
        ).astype(jnp.bfloat16)
        move(chunk, 0).start()

    for at in range(steps):
        for chunk in range(CHUNKS):
            move(chunk, at).wait_recv()
            taken = mask_ref[chunk, at][:, :1] > 0.5
            chosen = jnp.where(
                taken,
                landed[at, block(chunk)].astype(jnp.float32),
                held[at, block(chunk)].astype(jnp.float32),
            ).astype(jnp.bfloat16)
            if at < steps - 1:
                held[at + 1, block(chunk)] = chosen
                move(chunk, at + 1).start()
            else:
                out_ref[block(chunk)] = chosen

    for at in range(steps):
        for chunk in range(CHUNKS):
            move(chunk, at).wait_send()

    @pl.when(home)
    def _():
        for chunk in range(CHUNKS):
            raw_copy(chunk, 0).wait_send()
            raw_copy(chunk, 1).wait_send()
            sibling_copy(chunk).wait_send()

    @pl.when(jnp.logical_not(home))
    def _():
        for chunk in range(CHUNKS):
            for slot in range(2):
                for k in range(2):
                    final_copy(chunk, slot, k).wait_send()


def return_rows(part, tokens, masks):
    count, width = tokens.shape
    steps = len(ORDERS[0])
    shapes = [2, 3, 2, steps, steps]
    sems = [2, 2, 4, 2, 1, 1, steps, steps]
    return pl.pallas_call(
        return_kernel,
        name="return_rows",
        out_shape=jax.ShapeDtypeStruct(tokens.shape, tokens.dtype),
        in_specs=[VMEM] * 3,
        out_specs=VMEM,
        scratch_shapes=[pltpu.VMEM((n, count, width), jnp.bfloat16) for n in shapes]
        + [pltpu.SemaphoreType.DMA((n * CHUNKS,)) for n in sems],
        compiler_params=pltpu.CompilerParams(
            collective_id=2, has_side_effects=True, vmem_limit_bytes=48 * 2**20
        ),
    )(part, tokens, masks)


def rms_rows(values, gain_row):
    floats = values.astype(jnp.float32)
    scaled = lax.rsqrt(jnp.mean(floats * floats, axis=-1, keepdims=True) + epsilon)
    return floats * scaled * gain_row


def rotary(values, positions):
    half_size = values.shape[-1] // 2
    spread = jnp.arange(half_size, dtype=jnp.float32) * (2.0 / values.shape[-1])
    frequency = rope_base ** (-spread)
    angles = positions.astype(jnp.float32)[:, None] * frequency[None, :]
    cosine = jnp.cos(angles)[:, None, :]
    sine_part = jnp.sin(angles)[:, None, :]
    front_half = values[..., :half_size]
    back_half = values[..., half_size:]
    return jnp.concatenate(
        [front_half * cosine - back_half * sine_part, back_half * cosine + front_half * sine_part],
        axis=-1,
    )


def slot_layout(seq_lengths, row_count):
    ends_at = jnp.cumsum(seq_lengths)
    starts_at = ends_at - seq_lengths
    position = jnp.arange(row_count, dtype=jnp.int32)
    slot_of = jnp.sum((position[:, None] >= ends_at[None, :]).astype(jnp.int32), axis=1)
    onehot = (
        slot_of[:, None] == jnp.arange(seq_lengths.shape[0], dtype=jnp.int32)[None, :]
    ).astype(jnp.int32)
    within = position - jnp.sum(onehot * starts_at[None, :], axis=1)
    return (slot_of, within, onehot)


def attend(
    queries, own_keys, own_values, shared_keys, shared_values, slot_of, prefix_len, prompt_len
):
    row_count = queries.shape[0]
    head_size = queries.shape[-1]
    all_keys = jnp.concatenate([shared_keys, own_keys], axis=0)
    all_values = jnp.concatenate([shared_values, own_values], axis=0)
    shared_index = jnp.arange(shared_keys.shape[0], dtype=jnp.int32)
    shared_mask = ((shared_index // prompt_len)[None, :] == slot_of[:, None]) & (
        (shared_index % prompt_len)[None, :] < prefix_len[:, None]
    )
    position = jnp.arange(row_count, dtype=jnp.int32)
    own_mask = (slot_of[None, :] == slot_of[:, None]) & (position[None, :] <= position[:, None])
    allowed = jnp.concatenate([shared_mask, own_mask], axis=1)
    scores = jnp.einsum(
        "rgd,nd->grn", queries, all_keys, preferred_element_type=jnp.float32
    ) * head_size ** (-0.5)
    weights = jnp.where(allowed[None], jnp.exp(scores), 0.0)
    weighted = (weights / jnp.sum(weights, axis=-1, keepdims=True)).astype(jnp.bfloat16)
    blended = jnp.einsum("grn,nd->rgd", weighted, all_values, preferred_element_type=jnp.float32)
    return blended.reshape(row_count, -1).astype(jnp.bfloat16)


def shards(
    tokens,
    prompt_rows,
    norm_gain,
    w_query,
    w_key,
    w_value,
    w_out,
    q_gain,
    k_gain,
    seq_lengths,
    prompt_group,
    prompt_blocks,
    dest_offset,
):
    row_count, width = tokens.shape
    prompt_len = prompt_rows.shape[0]
    head_size = q_gain.shape[0]
    slot_count = seq_lengths.shape[0]
    depth = w_query.shape[0]
    groups = w_key.shape[1] // head_size
    rep = lax.axis_index("rep")

    halves = w_query.astype(jnp.bfloat16).reshape(depth, groups, 2, -1)
    key_cols = w_key.astype(jnp.bfloat16).reshape(depth, groups, 1, head_size)
    value_cols = w_value.astype(jnp.bfloat16).reshape(depth, groups, 1, head_size)
    win = jnp.concatenate([halves, jnp.concatenate([key_cols, value_cols], axis=2)], axis=3)
    win = win.transpose(1, 2, 0, 3).reshape(2 * groups, depth, -1)
    wout = w_out.astype(jnp.bfloat16).reshape(2 * groups, -1, depth).transpose(0, 2, 1)
    meta = jnp.concatenate([prompt_group, prompt_blocks]).astype(jnp.bfloat16)
    meta = jnp.pad(meta[None, :], ((0, META - 1), (0, width - 2 * slot_count)))
    rows, gin, gout = gather_all(jnp.concatenate([tokens, prompt_rows, meta], axis=0), win, wout)

    meta = rows[row_count + prompt_len, : 2 * slot_count].astype(jnp.int32)
    group_here, blocks_here = meta[:slot_count], meta[slot_count:]
    normed = rms_rows(rows[: row_count + prompt_len], norm_gain).astype(jnp.bfloat16)
    features = normed.shape[1]
    gin = gin.reshape(2, features, -1)
    left = jnp.dot(normed, gin[0], preferred_element_type=jnp.float32)
    right = jnp.dot(normed, gin[1], preferred_element_type=jnp.float32)
    half_width = left.shape[1] - head_size
    query_sum = jnp.concatenate([left[:row_count, :half_width], right[:row_count, :half_width]], axis=1)
    key_sum, values_all = left[:, half_width:], right[:, half_width:].astype(jnp.bfloat16)
    q_heads = query_sum.shape[1] // head_size

    slot_of, within, onehot = slot_layout(seq_lengths, row_count)
    prefix_len = jnp.sum(onehot * (blocks_here * PBLK)[None, :], axis=1)
    positions = prefix_len + within
    queries = rotary(rms_rows(query_sum.reshape(row_count, q_heads, head_size), q_gain), positions)
    queries = queries.astype(jnp.bfloat16)
    all_positions = jnp.concatenate([positions, jnp.arange(prompt_len, dtype=jnp.int32)])
    keys_all = rotary(rms_rows(key_sum[:, None], k_gain), all_positions).astype(jnp.bfloat16)[:, 0]
    shared = gather_prompts(
        jnp.concatenate([keys_all[row_count:], values_all[row_count:]], axis=1)
    ).reshape(-1, prompt_len, 2 * head_size)
    shared = jnp.concatenate(
        [lax.dynamic_index_in_dim(shared, group_here[j], 0, keepdims=False) for j in range(slot_count)],
        axis=0,
    )
    blended = attend(
        queries, keys_all[:row_count], values_all[:row_count],
        shared[:, :head_size], shared[:, head_size:], slot_of, prefix_len, prompt_len,
    )
    gout = gout.reshape(2, features, -1)
    half_rows = gout.shape[2]
    part = lax.dot_general(
        blended[:, :half_rows], gout[0], (((1,), (1,)), ((), ())), preferred_element_type=jnp.float32
    ) + lax.dot_general(
        blended[:, half_rows:], gout[1], (((1,), (1,)), ((), ())), preferred_element_type=jnp.float32
    )
    shift_rows = jnp.sum(onehot * dest_offset[None, :], axis=1)
    return return_rows(part.astype(jnp.bfloat16), tokens, move_masks(shift_rows, rep))


def solution(mesh):
    return jax.shard_map(
        shards,
        mesh=mesh,
        in_specs=(
            P("rep", "tp"),
            P("rep", "tp"),
            P(),
            P(("rep", "tp"), None),
            P(("rep", "tp"), None),
            P(("rep", "tp"), None),
            P(None, ("rep", "tp")),
            P(),
            P(),
            P(),
            P("rep"),
            P("rep"),
            P(),
        ),
        out_specs=P("rep", "tp"),
        check_vma=False,
    )
```

```python
import functools

import jax
import jax.numpy as jnp
from jax import lax
from jax.experimental import pallas as pl
from jax.experimental.pallas import tpu as pltpu
from jax.sharding import PartitionSpec as P

PBLK = 64
MESH = pl.DeviceIdType.MESH
ANY = pl.BlockSpec(memory_space=pl.ANY)
VMEM = pl.BlockSpec(memory_space=pltpu.VMEM)
OFFSETS = (0, -1, 1, 2)
META = 16

epsilon = 1e-06
rope_base = 1000000.0


def place():
    rep, tp = lax.axis_index("rep"), lax.axis_index("tp")
    return lax.rem(rep // 4, 4), (tp // 2) * 2 + rep // 16, lax.rem(rep, 4), lax.rem(tp, 2)


def device_at(x, y, z, core):
    return (lax.rem(y, 2) * 16 + x * 4 + z, (y // 2) * 2 + core)


def step(value, by):
    return lax.rem(value + (by + 4), 4)


def greet(peers):
    barrier = pltpu.get_barrier_semaphore()
    for peer in peers:
        pl.semaphore_signal(barrier, inc=1, device_id=peer, device_id_type=MESH)
    pl.semaphore_wait(barrier, len(peers))


def send(source, target, send_sem, recv_sem, device):
    return pltpu.make_async_remote_copy(
        src_ref=source,
        dst_ref=target,
        send_sem=send_sem,
        recv_sem=recv_sem,
        device_id=device,
        device_id_type=MESH,
    )


class Plane:
    COPIES = 72

    def __init__(self, view, send_sems, recv_sems):
        self.view, self.ss, self.rs = view, send_sems, recv_sems
        self.x, self.y, self.z, self.core = place()
        self.started = []

    def block(self, half, first, second, part=None):
        a, b = (first, second) if half == 0 else (second, first)
        return self.view(half, step(self.x, a) * 4 + step(self.z, b), part)

    def toward(self, half, phase, sign):
        if (phase == 0) == (half == 0):
            return device_at(step(self.x, sign), self.y, self.z, self.core)
        return device_at(self.x, self.y, step(self.z, sign), self.core)

    def copy(self, half, number, ref, device):
        at = half * 36 + number
        return send(ref, ref, self.ss.at[at], self.rs.at[at], device)

    def start(self, *args):
        made = self.copy(*args)
        made.start()
        self.started.append(made)

    def sibling(self):
        return device_at(self.x, self.y, self.z, 1 - self.core)

    def share(self, half, o1, o2):
        ref = self.block(half, OFFSETS[o1], OFFSETS[o2])
        self.start(half, 20 + 4 * o1 + o2, ref, self.sibling())

    def spread(self, half, o1):
        ref = self.block(half, OFFSETS[o1], 0)
        self.start(half, 4 + 4 * o1, ref, self.toward(half, 1, 1))
        self.start(half, 5 + 4 * o1, ref, self.toward(half, 1, -1))
        self.share(half, o1, 0)

    def begin(self):
        for half in range(2):
            ref = self.block(half, 0, 0)
            self.start(half, 0, ref, self.toward(half, 0, 1))
            self.start(half, 1, ref, self.toward(half, 0, -1))
        for half in range(2):
            self.spread(half, 0)

    def arrived(self, half, number, ref):
        self.copy(half, number, ref, self.sibling()).wait_recv()

    def first(self):
        for half in range(2):
            self.arrived(half, 0, self.block(half, -1, 0))
            self.start(half, 2, self.block(half, -1, 0, 0), self.toward(half, 0, 1))
            self.arrived(half, 1, self.block(half, 1, 0))
            self.start(half, 3, self.block(half, 1, 0, 1), self.toward(half, 0, -1))
        for half in range(2):
            self.spread(half, 1)
            self.spread(half, 2)

    def opposite(self):
        for half in range(2):
            self.arrived(half, 2, self.block(half, 2, 0, 0))
            self.arrived(half, 3, self.block(half, 2, 0, 1))
            self.spread(half, 3)

    def second(self, o1):
        off, base = OFFSETS[o1], 4 + 4 * o1
        for half in range(2):
            self.arrived(half, base, self.block(half, off, -1))
            self.start(half, base + 2, self.block(half, off, -1, 0), self.toward(half, 1, 1))
            self.arrived(half, base + 1, self.block(half, off, 1))
            self.start(half, base + 3, self.block(half, off, 1, 1), self.toward(half, 1, -1))
            self.share(half, o1, 1)
            self.share(half, o1, 2)

    def second_opposite(self, o1):
        off, base = OFFSETS[o1], 4 + 4 * o1
        for half in range(2):
            self.arrived(half, base + 2, self.block(half, off, 2, 0))
            self.arrived(half, base + 3, self.block(half, off, 2, 1))
            self.share(half, o1, 3)

    def rest(self):
        yield functools.partial(self.second, 0)
        for o1 in range(1, 4):
            yield functools.partial(self.second, o1)
            yield functools.partial(self.second_opposite, o1 - 1)
        yield functools.partial(self.second_opposite, 3)

    def second_all(self):
        for act in self.rest():
            act()

    def finish(self, shared_block):
        for half in range(2):
            for o1 in range(4):
                for o2 in range(4):
                    a, b = (o1, o2) if half == 0 else (o2, o1)
                    where = step(self.x, OFFSETS[a]) * 4 + step(self.z, OFFSETS[b])
                    self.arrived(half, 20 + 4 * o1 + o2, shared_block(half, where))
        for made in self.started:
            made.wait_send()


COLUMN = tuple((dy, dc) for dy in range(4) for dc in range(2) if (dy, dc) != (0, 0))


def column_peers():
    x, y, z, core = place()
    return [device_at(x, step(y, dy), z, core if dc == 0 else 1 - core) for dy, dc in COLUMN]


def plane_peers():
    x, y, z, core = place()
    peers = [device_at(step(x, s), y, z, core) for s in (1, -1)]
    return peers + [device_at(x, y, step(z, s), core) for s in (1, -1)]


class Column:
    def __init__(self, source, target, send_sems, recv_sems, local_sem, which):
        x, y, z, core = place()
        tp = lax.axis_index("tp")
        base = which * len(COLUMN)
        self.local = pltpu.make_async_copy(
            source.at[y * 2 + core], target.at[core, lax.rem(y, 2), x * 4 + z, tp], local_sem.at[which]
        )
        self.sent, self.got = [], []
        for n, (dy, dc) in enumerate(COLUMN):
            to_y, from_y = step(y, dy), step(y, -dy)
            peer_core = core if dc == 0 else 1 - core
            sems = send_sems.at[base + n], recv_sems.at[base + n]
            to = device_at(x, to_y, z, peer_core)
            slot = target.at[peer_core, lax.rem(y, 2), x * 4 + z, tp]
            self.sent.append(send(source.at[to_y * 2 + peer_core], slot, *sems, to))
            ref = target.at[core, lax.rem(from_y, 2), x * 4 + z, (from_y // 2) * 2 + peer_core]
            self.got.append(send(ref, ref, *sems, to))

    def start(self):
        self.local.start()
        for made in self.sent:
            made.start()

    def ready(self):
        self.local.wait()
        for made in self.got:
            made.wait_recv()

    def finish(self):
        for made in self.sent:
            made.wait_send()


def viewer(target, owner):
    def view(half, where, part=None):
        if part is None:
            return target.at[owner, half, where]
        return target.at[owner, half, where, pl.ds(part * 2, 2)]

    return view


def gather_kernel(
    x_ref, win_ref, wout_ref, rows_ref, other_ref, gin_ref, gout_ref,
    a_send, a_recv, in_send, in_recv, out_send, out_recv, t_send, t_recv, p_send, p_recv, local_sem,
):
    x, y, z, core = place()
    tp = lax.axis_index("tp")
    y_lo, y_hi = lax.rem(y, 2), y // 2
    sibling = device_at(x, y, z, 1 - core)
    greet(column_peers() + plane_peers())

    inward_rows = Column(win_ref, gin_ref, a_send, a_recv, local_sem, 0)
    outward_rows = Column(wout_ref, gout_ref, a_send, a_recv, local_sem, 1)
    inward_rows.start()
    outward_rows.start()

    count, width = x_ref.shape
    cut = count // 32 * 16

    def quarter(at):
        return pl.ds(pl.multiple_of(at * width, 128), width)

    def token_copy(number, source, target, device):
        return send(source, target, t_send.at[number], t_recv.at[number], device)

    def pass_on(number, at, source=None):
        ref = other_ref.at[:, quarter(at)]
        source = rows_ref.at[:, quarter(at)] if source is None else source
        return send(source, ref, p_send.at[number], p_recv.at[number], sibling)

    home = core == y_lo
    mine = rows_ref.at[:, quarter(tp)]
    up = send(x_ref, mine, t_send.at[0], t_recv.at[core], device_at(x, step(y, 1), z, y_lo))
    down = send(x_ref, mine, t_send.at[1], t_recv.at[2 + core], device_at(x, step(y, -1), z, y_lo))
    up.start()
    down.start()

    @pl.when(home)
    def _():
        pltpu.make_async_copy(x_ref, mine, local_sem.at[2]).start()
        pass_on(0, tp, x_ref).start()

    @pl.when(jnp.logical_not(home))
    def _():
        token_copy(4, x_ref, mine, sibling).start()
        pltpu.make_async_copy(x_ref, other_ref.at[:, quarter(tp)], local_sem.at[2]).start()

    inward = Plane(viewer(gin_ref, core), in_send, in_recv)
    outward = Plane(viewer(gout_ref, core), out_send, out_recv)
    inward_rows.ready()
    inward.begin()
    inward.first()
    inward.opposite()
    outward_rows.ready()
    outward.begin()

    def away_blocks():
        below, above = step(y, -1), step(y, 1)
        for k in range(2):
            low = (below // 2) * 2 + k
            high = (above // 2) * 2 + k
            yield k, low, high, below, above

    @pl.when(jnp.logical_not(home))
    def _():
        for k, low, high, below, above in away_blocks():
            ref = rows_ref.at[:, quarter(low)]
            token_copy(k, ref, ref, sibling).wait_recv()
            ref = rows_ref.at[pl.ds(0, cut), quarter(low)]
            token_copy(5 + k, ref, ref, device_at(x, above, z, core)).start()
            ref = rows_ref.at[:, quarter(high)]
            token_copy(2 + k, ref, ref, sibling).wait_recv()
            ref = rows_ref.at[pl.ds(cut, count - cut), quarter(high)]
            token_copy(7 + k, ref, ref, device_at(x, below, z, core)).start()
            pass_on(k, low).start()
            pass_on(2 + k, high).start()

    inward.second_all()
    outward.first()
    outward.opposite()
    outward.second_all()

    @pl.when(jnp.logical_not(home))
    def _():
        for k, low, high, below, above in away_blocks():
            ref = rows_ref.at[pl.ds(0, cut), quarter(low)]
            token_copy(5 + k, ref, ref, sibling).wait_send()
            ref = rows_ref.at[pl.ds(cut, count - cut), quarter(high)]
            token_copy(7 + k, ref, ref, sibling).wait_send()
            pass_on(k, low).wait_send()
            pass_on(2 + k, high).wait_send()
        token_copy(4, x_ref, mine, sibling).wait_send()
        pltpu.make_async_copy(x_ref, other_ref.at[:, quarter(tp)], local_sem.at[2]).wait()
        for number in (0, 2, 3):
            pass_on(number, tp).wait_recv()

    @pl.when(home)
    def _():
        opposite = 1 - y_hi
        for k in range(2):
            at = quarter(opposite * 2 + k)
            ref = rows_ref.at[pl.ds(0, cut), at]
            token_copy(5 + k, ref, ref, sibling).wait_recv()
            ref = rows_ref.at[pl.ds(cut, count - cut), at]
            token_copy(7 + k, ref, ref, sibling).wait_recv()
            pass_on(2 + k, opposite * 2 + k).start()
        ref = rows_ref.at[:, quarter(y_hi * 2 + 1 - core)]
        token_copy(4, ref, ref, sibling).wait_recv()
        pltpu.make_async_copy(x_ref, mine, local_sem.at[2]).wait()
        for number in range(4):
            pass_on(number, tp).wait_recv()
        pass_on(0, tp, x_ref).wait_send()
        for k in range(2):
            pass_on(2 + k, tp).wait_send()

    up.wait_send()
    down.wait_send()
    inward_rows.finish()
    outward_rows.finish()
    inward.finish(viewer(gin_ref, 1 - core))
    outward.finish(viewer(gout_ref, 1 - core))


def gather_all(rows, win, wout):
    count, width = rows.shape
    sems = [14, 14, Plane.COPIES, Plane.COPIES, Plane.COPIES, Plane.COPIES, 9, 9, 4, 4, 3]
    return pl.pallas_call(
        gather_kernel,
        name="gather_all",
        out_shape=(
            jax.ShapeDtypeStruct((count, 4 * width), rows.dtype),
            jax.ShapeDtypeStruct((count, 4 * width), rows.dtype),
            jax.ShapeDtypeStruct((2, 2, 16, 4) + win.shape[1:], win.dtype),
            jax.ShapeDtypeStruct((2, 2, 16, 4) + wout.shape[1:], wout.dtype),
        ),
        in_specs=[ANY] * 3,
        out_specs=(ANY,) * 4,
        scratch_shapes=[pltpu.SemaphoreType.DMA((n,)) for n in sems],
        compiler_params=pltpu.CompilerParams(collective_id=0, has_side_effects=True),
    )(rows, win, wout)


TILE = 64


def attend_kernel(
    q_ref, own_ref, prompt_ref, bounds_ref, group_ref, wout_ref, out_ref, gout_ref,
    prompts, shared, total, sums, a_send, a_recv, out_send, out_recv, kv_send, kv_recv, local_sem,
):
    x, y, z, core = place()
    head = prompt_ref.shape[1] // 2
    heads = q_ref.shape[0]
    greet(column_peers() + plane_peers())
    mine = pltpu.make_async_copy(prompt_ref, prompts.at[core * 16 + x * 4 + z], local_sem.at[1])
    mine.start()
    rows = Column(wout_ref, gout_ref, a_send, a_recv, local_sem, 0)
    rows.start()
    mine.wait()

    def prompt_viewer(owner):
        def view(half, where, part=None):
            span = pl.ds(half * 64, 64) if part is None else pl.ds(half * 64 + part * 32, 32)
            return prompts.at[owner * 16 + where, span]

        return view

    kv = Plane(prompt_viewer(core), kv_send, kv_recv)
    outward = Plane(viewer(gout_ref, core), out_send, out_recv)
    kv.begin()
    scale = head ** (-0.5) * 1.4426950408889634

    def weigh(tile, keys, values, low, high):
        span = pl.ds(tile * TILE, TILE)
        queries = q_ref[:, span].reshape(heads * TILE, head)
        scores = lax.dot_general(
            queries, keys, (((1,), (1,)), ((), ())), preferred_element_type=jnp.float32
        )
        count = keys.shape[0]
        at = lax.broadcasted_iota(jnp.int32, (TILE, count), 1)
        allowed = (at >= low) & (at < high)
        weights = jnp.where(
            allowed[None], jnp.exp2(scores.reshape(heads, TILE, count) * scale), 0.0
        )
        blend = jnp.dot(
            weights.astype(jnp.bfloat16).reshape(heads * TILE, count), values,
            preferred_element_type=jnp.float32,
        )
        return span, jnp.sum(weights, axis=-1, keepdims=True), blend.reshape(heads, TILE, head)

    def own_tile(tile):
        span = slice(tile * TILE, (tile + 1) * TILE)
        count = min(-(-(tile + 1) * TILE // 128) * 128, own_ref.shape[0])
        low = bounds_ref[span, 0:1]
        high = lax.broadcasted_iota(jnp.int32, (TILE, 1), 0) + (tile * TILE + 1)
        span, weight, blend = weigh(tile, own_ref[:count, :head], own_ref[:count, head:], low, high)
        total[:, span] = blend
        sums[:, span] = jnp.broadcast_to(weight, (heads, TILE, head))

    def shared_tile(tile):
        span = slice(tile * TILE, (tile + 1) * TILE)
        low, high = bounds_ref[span, 1:2], bounds_ref[span, 2:3]
        span, weight, blend = weigh(tile, shared[:, :head], shared[:, head:], low, high)
        blend = (total[:, span] + blend) / (sums[:, span] + weight)
        for h in range(heads):
            out_ref[span, h * head : (h + 1) * head] = blend[h].astype(jnp.bfloat16)

    tiles = q_ref.shape[1] // TILE
    for tile in range(4):
        own_tile(tile)
    rows.ready()
    kv.first()
    outward.begin()
    own_tile(4)
    kv.opposite()
    own_tile(5)
    kv.second(0)
    outward.first()
    own_tile(6)
    acts = list(kv.rest())[1:]
    for act in acts[:3]:
        act()
    outward.opposite()
    for act in acts[3:]:
        act()
    kv.finish(prompt_viewer(1 - core))
    for j in range(group_ref.shape[0]):
        shared[j * prompts.shape[1] : (j + 1) * prompts.shape[1]] = prompts[group_ref[j]]
    later = list(outward.rest())
    for tile in range(tiles):
        later[tile]()
        shared_tile(tile)
    for act in later[tiles:]:
        act()
    rows.finish()
    outward.finish(viewer(gout_ref, 1 - core))


def attend(queries, own, prompt, bounds, group, wout):
    heads, count, head = queries.shape
    sems = [7, 7, Plane.COPIES, Plane.COPIES, Plane.COPIES, Plane.COPIES, 2]
    return pl.pallas_call(
        attend_kernel,
        name="attend",
        out_shape=(
            jax.ShapeDtypeStruct((count, heads * head), jnp.bfloat16),
            jax.ShapeDtypeStruct((2, 2, 16, 4) + wout.shape[1:], wout.dtype),
        ),
        in_specs=[VMEM] * 4 + [pl.BlockSpec(memory_space=pltpu.SMEM), ANY],
        out_specs=(VMEM, ANY),
        scratch_shapes=[
            pltpu.VMEM((32,) + prompt.shape, prompt.dtype),
            pltpu.VMEM((group.shape[0] * prompt.shape[0], prompt.shape[1]), prompt.dtype),
            pltpu.VMEM(queries.shape, jnp.float32),
            pltpu.VMEM(queries.shape, jnp.float32),
        ]
        + [pltpu.SemaphoreType.DMA((n,)) for n in sems],
        compiler_params=pltpu.CompilerParams(
            collective_id=1, has_side_effects=True, vmem_limit_bytes=48 * 2**20
        ),
    )(queries, own, prompt, bounds, group, wout)


BLOCK = 128
LEVELS = ("z1", "x1", "z2", "x2")


def level_bits(shift, sign):
    odd = shift % 2 == 1
    far = (shift >= 2) if sign == 1 else ((shift == 1) | (shift == 2))
    return odd, far


def along_z(shift, z):
    return shift % 4, shift // 4 + (z < shift % 4).astype(jnp.int32)


def y_shift(shift, x, z):
    shift_z, need_x = along_z(shift, (z + shift) % 4)
    end_x = (x + need_x) % 4
    return (need_x // 4 + (end_x < need_x % 4).astype(jnp.int32)) % 2 == 1


def move_masks(shift, x, z):
    masks = []
    for sign in (1, -1):
        odd_z, far_z = level_bits(shift % 4, sign)
        for level in LEVELS:
            end_z = (z + (2 * far_z.astype(jnp.int32) if level in ("z1", "x1") else 0)) % 4
            odd_x, far_x = level_bits(along_z(shift, end_z)[1] % 4, sign)
            masks.append({"z1": odd_z, "x1": odd_x, "z2": far_z, "x2": far_x}[level])
    masks = jnp.stack(masks).astype(jnp.float32)
    return jnp.broadcast_to(masks[:, :, None], masks.shape + (BLOCK,))


def return_kernel(
    blend_ref, w0_ref, w1_ref, residual_ref, mask_ref, out_ref,
    sums, source, home_sum, home_got, raw, final, held, landed,
    src_send, raw_recv, fin_recv, move_send, move_recv,
):
    x, y, z, core = place()
    y_lo, y_hi = lax.rem(y, 2), y // 2
    width = out_ref.shape[1]
    blocks = width // BLOCK
    above, below = step(y, 1), step(y, -1)
    sibling = device_at(x, y, z, 1 - core)
    peers = [device_at(x, at, z, k) for at in (above, below) for k in range(2)] + [sibling]
    peers += [device_at(step(x, s), y, z, core) for s in (1, -1, 2)]
    peers += [device_at(x, y, step(z, s), core) for s in (1, -1, 2)]
    greet(peers)
    home = core == y_lo
    away = jnp.logical_not(home)

    far, up, down = 1 - y_hi, above // 2, below // 2
    quarters = (
        jnp.where(home, far * 2, up * 2),
        jnp.where(home, far * 2 + 1, down * 2 + 1),
        jnp.where(home, y_hi * 2 + 1 - core, up * 2 + 1),
        jnp.where(home, y_hi * 2 + core, down * 2),
    )
    pieces = w0_ref.shape[0]
    depth = w0_ref.shape[2]

    def raw_copy(j, slot):
        to = device_at(x, (above, below)[slot], z, core)
        at = slot * blocks + j
        return send(source.at[slot, j], raw.at[slot, j], src_send.at[at], raw_recv.at[at], to)

    def sibling_copy(j):
        at = 2 * blocks + j
        return send(home_sum.at[j], home_got.at[j], src_send.at[at], fin_recv.at[at], sibling)

    def final_copy(j, at):
        slot, k = ((0, 0), (1, 1), (0, 1), (1, 0))[at]
        to = device_at(x, (above, below)[slot], z, k)
        return send(
            source.at[at, j], final.at[slot, j],
            src_send.at[at * blocks + j], fin_recv.at[slot * blocks + j], to,
        )

    def multiply(pair):
        for at in range(4):
            start = pl.multiple_of(quarters[at] * width + pair * 2 * BLOCK, 2 * BLOCK)
            total = None
            for half in range(pieces):
                for n, w_ref in enumerate((w0_ref, w1_ref)):
                    column = (half * 2 + n) * depth
                    term = lax.dot_general(
                        blend_ref[:, column : column + depth], w_ref[half, pl.ds(start, 2 * BLOCK)],
                        (((1,), (1,)), ((), ())), preferred_element_type=jnp.float32,
                    )
                    total = term if total is None else total + term
            sums[at] = total
        lanes = [pl.ds(i * BLOCK, BLOCK) for i in range(2)]

        @pl.when(home)
        def _():
            for i in range(2):
                j = pair * 2 + i
                for slot in range(2):
                    source[slot, j] = sums[slot, :, lanes[i]].astype(jnp.bfloat16)
                    raw_copy(j, slot).start()
            for i in range(2):
                j = pair * 2 + i
                theirs = pl.ds(pl.multiple_of((1 - core) * width + j * BLOCK, BLOCK), BLOCK)
                home_sum[j] = sums[2, :, lanes[i]] + residual_ref[:, theirs].astype(jnp.float32)
                sibling_copy(j).start()
                mine = pl.ds(pl.multiple_of(core * width + j * BLOCK, BLOCK), BLOCK)
                home_got[j] = sums[3, :, lanes[i]] + residual_ref[:, mine].astype(jnp.float32)

        @pl.when(away)
        def _():
            for i in range(2):
                j = pair * 2 + i
                for at in (2, 3):
                    source[at, j] = sums[at, :, lanes[i]].astype(jnp.bfloat16)
                    final_copy(j, at).start()
            for i in range(2):
                j = pair * 2 + i
                for at in range(2):
                    partial[at, j] = sums[at, :, lanes[i]].astype(jnp.bfloat16)

    partial = source

    def add(j):
        @pl.when(away)
        def _():
            for slot in range(2):
                raw_copy(j, slot).wait_recv()
                source[slot, j] = (
                    partial[slot, j].astype(jnp.float32) + raw[slot, j].astype(jnp.float32)
                ).astype(jnp.bfloat16)
                final_copy(j, slot).start()

    def move(j, level):
        by = (1, -1)[j % 2] if LEVELS[level][1] == "1" else 2
        if LEVELS[level][0] == "z":
            to = device_at(x, y, step(z, by), core)
        else:
            to = device_at(step(x, by), y, z, core)
        at = level * blocks + j
        return send(
            held.at[level, j], landed.at[level, j], move_send.at[at], move_recv.at[at], to
        )

    def finish(j):
        for slot in range(2):
            final_copy(j, slot).wait_recv()

        @pl.when(away)
        def _():
            sibling_copy(j).wait_recv()

        total = final[0, j].astype(jnp.float32) + final[1, j].astype(jnp.float32) + home_got[j]
        held[0, j] = total.astype(jnp.bfloat16)
        move(j, 0).start()

    def take(j, level):
        move(j, level).wait_recv()
        chosen = jnp.where(
            mask_ref[(j % 2) * len(LEVELS) + level] > 0.5,
            landed[level, j].astype(jnp.float32),
            held[level, j].astype(jnp.float32),
        ).astype(jnp.bfloat16)
        if level + 1 < len(LEVELS):
            held[level + 1, j] = chosen
            move(j, level + 1).start()
        else:
            out_ref[:, j * BLOCK : (j + 1) * BLOCK] = chosen

    for tick in range(blocks + 2 + len(LEVELS)):
        if tick < blocks // 2:
            multiply(tick)
        for j in range(blocks):
            if tick == j + 1:
                add(j)
        for j in range(blocks):
            if tick == j + 2:
                finish(j)
        for level in reversed(range(len(LEVELS))):
            j = tick - 3 - level
            if 0 <= j < blocks:
                take(j, level)

    for j in range(blocks):
        for level in range(len(LEVELS)):
            move(j, level).wait_send()

        @pl.when(home)
        def _():
            raw_copy(j, 0).wait_send()
            raw_copy(j, 1).wait_send()
            sibling_copy(j).wait_send()

        @pl.when(away)
        def _():
            for at in range(4):
                final_copy(j, at).wait_send()


def return_rows(blended, w0, w1, residual, masks):
    count = blended.shape[0]
    width = residual.shape[1] // 2
    blocks = width // BLOCK
    levels = len(LEVELS)

    def room(n, dtype=jnp.bfloat16):
        return pltpu.VMEM((n, blocks, count, BLOCK), dtype)

    return pl.pallas_call(
        return_kernel,
        name="return_rows",
        out_shape=jax.ShapeDtypeStruct((count, width), jnp.bfloat16),
        in_specs=[VMEM] * 5,
        out_specs=VMEM,
        scratch_shapes=[
            pltpu.VMEM((4, count, 2 * BLOCK), jnp.float32),
            room(4),
            pltpu.VMEM((blocks, count, BLOCK), jnp.float32),
            pltpu.VMEM((blocks, count, BLOCK), jnp.float32),
            room(2),
            room(2),
            room(levels),
            room(levels),
        ]
        + [pltpu.SemaphoreType.DMA((n * blocks,)) for n in (4, 2, 3, levels, levels)],
        compiler_params=pltpu.CompilerParams(
            collective_id=2, has_side_effects=True, vmem_limit_bytes=56 * 2**20
        ),
    )(blended, w0, w1, residual, masks)


def rms_rows(values, gain_row):
    floats = values.astype(jnp.float32)
    scaled = lax.rsqrt(jnp.mean(floats * floats, axis=-1, keepdims=True) + epsilon)
    return floats * scaled * gain_row


def rotary(values, positions):
    half_size = values.shape[-1] // 2
    spread = jnp.arange(half_size, dtype=jnp.float32) * (2.0 / values.shape[-1])
    frequency = rope_base ** (-spread)
    angles = positions.astype(jnp.float32)[:, None] * frequency[None, :]
    cosine = jnp.cos(angles)[:, None, :]
    sine_part = jnp.sin(angles)[:, None, :]
    front_half = values[..., :half_size]
    back_half = values[..., half_size:]
    return jnp.concatenate(
        [front_half * cosine - back_half * sine_part, back_half * cosine + front_half * sine_part],
        axis=-1,
    )


def slot_layout(seq_lengths, row_count):
    ends_at = jnp.cumsum(seq_lengths)
    starts_at = ends_at - seq_lengths
    position = jnp.arange(row_count, dtype=jnp.int32)
    slot_of = jnp.sum((position[:, None] >= ends_at[None, :]).astype(jnp.int32), axis=1)
    onehot = (
        slot_of[:, None] == jnp.arange(seq_lengths.shape[0], dtype=jnp.int32)[None, :]
    ).astype(jnp.int32)
    within = position - jnp.sum(onehot * starts_at[None, :], axis=1)
    return (slot_of, within, onehot)


def shards(
    tokens,
    prompt_rows,
    norm_gain,
    w_query,
    w_key,
    w_value,
    w_out,
    q_gain,
    k_gain,
    seq_lengths,
    prompt_group,
    prompt_blocks,
    dest_offset,
):
    row_count, width = tokens.shape
    prompt_len = prompt_rows.shape[0]
    head_size = q_gain.shape[0]
    slot_count = seq_lengths.shape[0]
    depth = w_query.shape[0]
    groups = w_key.shape[1] // head_size
    rep = lax.axis_index("rep")

    halves = w_query.astype(jnp.bfloat16).reshape(depth, groups, 2, -1)
    key_cols = w_key.astype(jnp.bfloat16).reshape(depth, groups, 1, head_size)
    value_cols = w_value.astype(jnp.bfloat16).reshape(depth, groups, 1, head_size)
    win = jnp.concatenate([halves, jnp.concatenate([key_cols, value_cols], axis=2)], axis=3)
    win = win.transpose(1, 2, 0, 3).reshape(2 * groups, depth, -1)
    wout = w_out.astype(jnp.bfloat16).reshape(2 * groups, 2, -1, depth).transpose(1, 0, 3, 2)
    meta = jnp.concatenate([prompt_group, prompt_blocks]).astype(jnp.bfloat16)
    meta = jnp.pad(meta[None, :], ((0, META - 1), (0, width - 2 * slot_count)))
    rows, other, gin, gout = gather_all(
        jnp.concatenate([tokens, prompt_rows, meta], axis=0), win, wout[0]
    )

    plane_x, plane_z = rep // 4 % 4, rep % 4
    slot_of, within, onehot = slot_layout(seq_lengths, row_count)
    crosses = y_shift(dest_offset, plane_x, plane_z)
    pair = jnp.stack([rows[row_count + prompt_len], other[row_count + prompt_len]])
    pair = pair[:, : 2 * slot_count].astype(jnp.int32).reshape(2, 2, slot_count)
    group_here, blocks_here = jnp.where(crosses, pair[1], pair[0])
    shift_rows = jnp.sum(onehot * dest_offset[None, :], axis=1)
    row_crosses = jnp.sum(onehot * crosses[None, :], axis=1) == 1
    inputs = jnp.where(row_crosses[:, None], other[:row_count], rows[:row_count])
    normed = rms_rows(
        jnp.concatenate([inputs, rows[row_count : row_count + prompt_len]], axis=0), norm_gain
    ).astype(jnp.bfloat16)
    features = normed.shape[1]
    gin = gin.reshape(2, features, -1)
    left = jnp.dot(normed, gin[0], preferred_element_type=jnp.float32)
    right = jnp.dot(normed, gin[1], preferred_element_type=jnp.float32)
    half_width = left.shape[1] - head_size
    query_sum = jnp.concatenate([left[:row_count, :half_width], right[:row_count, :half_width]], axis=1)
    key_sum, values_all = left[:, half_width:], right[:, half_width:].astype(jnp.bfloat16)
    q_heads = query_sum.shape[1] // head_size

    prefix_len = jnp.sum(onehot * (blocks_here * PBLK)[None, :], axis=1)
    positions = prefix_len + within
    queries = rotary(rms_rows(query_sum.reshape(row_count, q_heads, head_size), q_gain), positions)
    queries = queries.astype(jnp.bfloat16).transpose(1, 0, 2)
    all_positions = jnp.concatenate([positions, jnp.arange(prompt_len, dtype=jnp.int32)])
    keys_all = rotary(rms_rows(key_sum[:, None], k_gain), all_positions).astype(jnp.bfloat16)[:, 0]
    pairs = jnp.concatenate([keys_all, values_all], axis=1)
    bounds = jnp.stack(
        [jnp.arange(row_count, dtype=jnp.int32) - within, slot_of * prompt_len, slot_of * prompt_len + prefix_len], axis=1
    )
    bounds = jnp.pad(bounds, ((0, 0), (0, head_size - 3)))
    blended, gout_b = attend(
        queries, pairs[:row_count], pairs[row_count:], bounds, group_here, wout[1]
    )
    gout, gout_b = gout.reshape(2, features, -1), gout_b.reshape(2, features, -1)
    residual = lax.dynamic_slice_in_dim(
        inputs, lax.axis_index("tp") // 2 * (2 * width), 2 * width, axis=1
    )
    return return_rows(
        blended, gout, gout_b, residual,
        move_masks(shift_rows, plane_x, plane_z),
    )


def solution(mesh):
    return jax.shard_map(
        shards,
        mesh=mesh,
        in_specs=(
            P("rep", "tp"),
            P("rep", "tp"),
            P(),
            P(("rep", "tp"), None),
            P(("rep", "tp"), None),
            P(("rep", "tp"), None),
            P(None, ("rep", "tp")),
            P(),
            P(),
            P(),
            P("rep"),
            P("rep"),
            P(),
        ),
        out_specs=P("rep", "tp"),
        check_vma=False,
    )
```

```python
import functools

import jax
import jax.numpy as jnp
import numpy as np
from jax import lax
from jax.experimental import pallas as pl
from jax.experimental.pallas import tpu as pltpu
from jax.sharding import PartitionSpec as P

PBLK = 64
PBLOCKS = 2
MESH = pl.DeviceIdType.MESH
ANY = pl.BlockSpec(memory_space=pl.ANY)
VMEM = pl.BlockSpec(memory_space=pltpu.VMEM)
OFFSETS = (0, -1, 1, 2)
META = 16
CROSS, START, PROMPT, SLOT, WITHIN, MOVES = 0, 1, 2, 3, 4, 8
EARLY = 128

epsilon = 1e-06
rope_base = 1000000.0


def place():
    rep, tp = lax.axis_index("rep"), lax.axis_index("tp")
    return lax.rem(rep // 4, 4), (tp // 2) * 2 + rep // 16, lax.rem(rep, 4), lax.rem(tp, 2)


def device_at(x, y, z, core):
    return (lax.rem(y, 2) * 16 + x * 4 + z, (y // 2) * 2 + core)


def step(value, by):
    return lax.rem(value + (by + 4), 4)


def greet(peers):
    barrier = pltpu.get_barrier_semaphore()
    for peer in peers:
        pl.semaphore_signal(barrier, inc=1, device_id=peer, device_id_type=MESH)
    pl.semaphore_wait(barrier, len(peers))


def send(source, target, send_sem, recv_sem, device):
    return pltpu.make_async_remote_copy(
        src_ref=source,
        dst_ref=target,
        send_sem=send_sem,
        recv_sem=recv_sem,
        device_id=device,
        device_id_type=MESH,
    )


class Plane:
    COPIES = 72

    def __init__(self, view, send_sems, recv_sems):
        self.view, self.ss, self.rs = view, send_sems, recv_sems
        self.x, self.y, self.z, self.core = place()
        self.started = []

    def block(self, half, first, second, part=None):
        a, b = (first, second) if half == 0 else (second, first)
        return self.view(half, step(self.x, a) * 4 + step(self.z, b), part)

    def toward(self, half, phase, sign):
        if (phase == 0) == (half == 0):
            return device_at(step(self.x, sign), self.y, self.z, self.core)
        return device_at(self.x, self.y, step(self.z, sign), self.core)

    def copy(self, half, number, ref, device):
        at = half * 36 + number
        return send(ref, ref, self.ss.at[at], self.rs.at[at], device)

    def start(self, *args):
        made = self.copy(*args)
        made.start()
        self.started.append(made)

    def sibling(self):
        return device_at(self.x, self.y, self.z, 1 - self.core)

    def share(self, half, o1, o2):
        ref = self.block(half, OFFSETS[o1], OFFSETS[o2])
        self.start(half, 20 + 4 * o1 + o2, ref, self.sibling())

    def spread(self, half, o1):
        ref = self.block(half, OFFSETS[o1], 0)
        self.start(half, 4 + 4 * o1, ref, self.toward(half, 1, 1))
        self.start(half, 5 + 4 * o1, ref, self.toward(half, 1, -1))
        self.share(half, o1, 0)

    def begin(self):
        for half in range(2):
            ref = self.block(half, 0, 0)
            self.start(half, 0, ref, self.toward(half, 0, 1))
            self.start(half, 1, ref, self.toward(half, 0, -1))
        for half in range(2):
            self.spread(half, 0)

    def arrived(self, half, number, ref):
        self.copy(half, number, ref, self.sibling()).wait_recv()

    def first(self):
        for half in range(2):
            self.arrived(half, 0, self.block(half, -1, 0))
            self.start(half, 2, self.block(half, -1, 0, 0), self.toward(half, 0, 1))
            self.arrived(half, 1, self.block(half, 1, 0))
            self.start(half, 3, self.block(half, 1, 0, 1), self.toward(half, 0, -1))
        for half in range(2):
            self.spread(half, 1)
            self.spread(half, 2)

    def opposite(self):
        for half in range(2):
            self.arrived(half, 2, self.block(half, 2, 0, 0))
            self.arrived(half, 3, self.block(half, 2, 0, 1))
            self.spread(half, 3)

    def second(self, o1):
        off, base = OFFSETS[o1], 4 + 4 * o1
        for half in range(2):
            self.arrived(half, base, self.block(half, off, -1))
            self.start(half, base + 2, self.block(half, off, -1, 0), self.toward(half, 1, 1))
            self.arrived(half, base + 1, self.block(half, off, 1))
            self.start(half, base + 3, self.block(half, off, 1, 1), self.toward(half, 1, -1))
            self.share(half, o1, 1)
            self.share(half, o1, 2)

    def second_opposite(self, o1):
        off, base = OFFSETS[o1], 4 + 4 * o1
        for half in range(2):
            self.arrived(half, base + 2, self.block(half, off, 2, 0))
            self.arrived(half, base + 3, self.block(half, off, 2, 1))
            self.share(half, o1, 3)

    def rest(self):
        yield functools.partial(self.second, 0)
        for o1 in range(1, 4):
            yield functools.partial(self.second, o1)
            yield functools.partial(self.second_opposite, o1 - 1)
        yield functools.partial(self.second_opposite, 3)

    def second_all(self):
        for act in self.rest():
            act()

    def finish(self, shared_block):
        for half in range(2):
            for o1 in range(4):
                for o2 in range(4):
                    a, b = (o1, o2) if half == 0 else (o2, o1)
                    where = step(self.x, OFFSETS[a]) * 4 + step(self.z, OFFSETS[b])
                    self.arrived(half, 20 + 4 * o1 + o2, shared_block(half, where))
        for made in self.started:
            made.wait_send()


COLUMN = tuple((dy, dc) for dy in range(4) for dc in range(2) if (dy, dc) != (0, 0))


def column_peers():
    x, y, z, core = place()
    return [device_at(x, step(y, dy), z, core if dc == 0 else 1 - core) for dy, dc in COLUMN]


def plane_peers():
    x, y, z, core = place()
    peers = [device_at(step(x, s), y, z, core) for s in (1, -1)]
    return peers + [device_at(x, y, step(z, s), core) for s in (1, -1)]


class Column:
    def __init__(self, source, land, send_sems, recv_sems, local_sem, which):
        x, y, z, core = place()
        tp = lax.axis_index("tp")
        base = which * len(COLUMN)
        y_lo = lax.rem(y, 2)
        self.local = pltpu.make_async_copy(
            source.at[y * 2 + core], land(core, y_lo, tp), local_sem.at[which]
        )
        self.sent, self.got = [], []
        for n, (dy, dc) in enumerate(COLUMN):
            to_y, from_y = step(y, dy), step(y, -dy)
            peer = core if dc == 0 else 1 - core
            sems = send_sems.at[base + n], recv_sems.at[base + n]
            to = device_at(x, to_y, z, peer)
            self.sent.append(send(source.at[to_y * 2 + peer], land(peer, y_lo, tp), *sems, to))
            ref = land(core, lax.rem(from_y, 2), (from_y // 2) * 2 + peer)
            self.got.append(send(ref, ref, *sems, to))

    def start(self):
        self.local.start()
        for made in self.sent:
            made.start()

    def ready(self):
        self.local.wait()
        for made in self.got:
            made.wait_recv()

    def finish(self):
        for made in self.sent:
            made.wait_send()


def lander(target):
    x, _, z, _ = place()
    return lambda core, y_lo, tp: target.at[core, y_lo, x * 4 + z, tp]


def viewer(target, owner):
    def view(half, where, part=None):
        if part is None:
            return target.at[owner, half, where]
        return target.at[owner, half, where, pl.ds(part * 2, 2)]

    return view


def project_kernel(
    tokens_ref, prompt_ref, marks_ref, win_ref, wout_ref, info_ref, gain_ref, head_gain_ref, turn_ref,
    q_ref, pairs_ref, residual_ref, prefix_ref, meta_ref, gout_ref,
    x_ref, rows, theirs, gin, stage, scaled, sums, squares, turn,
    a_send, a_recv, in_send, in_recv, out_send, out_recv, t_send, t_recv, p_send, p_recv, local_sem,
):
    x, y, z, core = place()
    tp = lax.axis_index("tp")
    y_lo, y_hi = lax.rem(y, 2), y // 2
    sibling = device_at(x, y, z, 1 - core)
    above, below = step(y, 1), step(y, -1)
    row_count = residual_ref.shape[0]
    loads, at = [], 0
    for n, ref in enumerate((tokens_ref, prompt_ref, marks_ref)):
        loads.append(
            pltpu.make_async_copy(ref, x_ref.at[pl.ds(at, ref.shape[0])], local_sem.at[3 + n])
        )
        at += ref.shape[0]
    for load in loads:
        load.start()
    greet(column_peers() + plane_peers())
    inward_rows = Column(
        win_ref, lambda _, lo, at: stage.at[lo, at], a_send, a_recv, local_sem, 0
    )
    outward_rows = Column(wout_ref, lander(gout_ref), a_send, a_recv, local_sem, 1)
    inward_rows.start()
    outward_rows.start()
    for load in loads:
        load.wait()

    count, width = x_ref.shape
    cut = count // 32 * 16
    parts = (pl.ds(0, cut), pl.ds(cut, count - cut))
    home = core == y_lo
    away = jnp.logical_not(home)

    def quarter(at):
        return pl.ds(pl.multiple_of(at * width, 128), width)

    def own_part(up, part):
        to = device_at(x, above if up else below, z, y_lo)
        at = (0 if up else 4) + core * 2 + part
        ref = rows.at[parts[part], quarter(tp)]
        return send(x_ref.at[parts[part]], ref, t_send.at[(0 if up else 2) + part], t_recv.at[at], to)

    def token_copy(number, ref, device, source=None):
        source = ref if source is None else source
        return send(source, ref, t_send.at[number], t_recv.at[number], device)

    def pass_on(i):
        source = rows.at[pl.ds(0, row_count), quarter(y_hi * 2 + i)]
        target = theirs.at[:, pl.ds(i * width, width)]
        return send(source, target, p_send.at[i], p_recv.at[i], sibling)

    mine = rows.at[:, quarter(tp)]
    keep = pltpu.make_async_copy(x_ref, mine, local_sem.at[2])
    own_parts = [own_part(True, 0), own_part(False, 1), own_part(True, 1), own_part(False, 0)]
    for made in own_parts:
        made.start()

    @pl.when(home)
    def _():
        keep.start()

    @pl.when(away)
    def _():
        token_copy(8, mine, sibling, x_ref).start()

    def gin_viewer(owner):
        size = stage.shape[1] * stage.shape[2]

        def view(half, where, part=None):
            start = (half * 16 + where) * size
            if part is None:
                return gin.at[owner, pl.ds(pl.multiple_of(start, 16), size)]
            start = start + part * (size // 2)
            return gin.at[owner, pl.ds(pl.multiple_of(start, 16), size // 2)]

        return view

    inward = Plane(gin_viewer(core), in_send, in_recv)
    outward = Plane(viewer(gout_ref, core), out_send, out_recv)
    inward_rows.ready()
    for half in range(2):
        block = stage[half].astype(jnp.float32)
        inward.block(half, 0, 0)[...] = block.reshape(-1, block.shape[-1]).astype(jnp.bfloat16)
    inward.begin()
    inward.first()
    inward.opposite()
    outward_rows.ready()
    outward.begin()
    row_tile = 64
    acts = list(inward.rest())

    def fill_turns(tile):
        lane = lax.broadcasted_iota(jnp.int32, (row_tile, turn.shape[3]), 1)
        sign = jnp.where(lane < turn.shape[3] // 2, -1.0, 1.0)
        span = slice(tile * row_tile, (tile + 1) * row_tile)
        if tile * row_tile < row_count:
            starts = [info_ref[span, WITHIN : WITHIN + 1] + PBLK * (n + 1) for n in range(PBLOCKS)]
        else:
            first = lax.broadcasted_iota(jnp.int32, (row_tile, 1), 0).astype(jnp.float32)
            starts = [first + (tile * row_tile - row_count)]
        for n, start in enumerate(starts):
            angles = start * turn_ref[0:1]
            turn[n, 0, span] = jnp.cos(angles)
            turn[n, 1, span] = jnp.sin(angles) * sign

    fill_turns(0)
    fill_turns(1)
    for act in acts[:3]:
        act()
        fill_turns(acts.index(act) + 2)

    low, high = (below // 2) * 2, (above // 2) * 2

    @pl.when(away)
    def _():
        for k in range(2):
            ref = rows.at[parts[0], quarter(low + k)]
            token_copy(k * 2, ref, sibling).wait_recv()
            token_copy(9 + k, ref, device_at(x, above, z, core)).start()
            ref = rows.at[parts[1], quarter(high + k)]
            token_copy(4 + k * 2 + 1, ref, sibling).wait_recv()
            token_copy(11 + k, ref, device_at(x, below, z, core)).start()

    for n, act in enumerate(acts[3:]):
        act()
        if n < 4:
            fill_turns(n + 5)
    outward.first()
    inward.finish(gin_viewer(1 - core))
    outward.opposite()
    later = list(outward.rest())

    def multiply(i):
        at = quarter(y_hi * 2 + i if i < 2 else (1 - y_hi) * 2 + i - 2)
        gain = gain_ref[:, at]
        for tile in range(scaled.shape[0] // row_tile):
            span = pl.ds(tile * row_tile, row_tile)
            values = rows[span, at].astype(jnp.float32)
            total = jnp.sum(values * values, axis=1, keepdims=True)
            total = jnp.broadcast_to(total, (row_tile, squares.shape[1]))
            squares[span] = total if i == 0 else squares[span] + total
            scaled[span] = (values * gain).astype(jnp.bfloat16)
        for half in range(2):
            term = jnp.dot(scaled[...], gin[half, at], preferred_element_type=jnp.float32)
            sums[half] = term if i == 0 else sums[half] + term

    @pl.when(away)
    def _():
        for k in range(2):
            token_copy(k * 2 + 1, rows.at[parts[1], quarter(low + k)], sibling).wait_recv()
            token_copy(4 + k * 2, rows.at[parts[0], quarter(high + k)], sibling).wait_recv()
        for i in range(2):
            pass_on(i).start()

    @pl.when(home)
    def _():
        keep.wait()
        token_copy(8, rows.at[:, quarter(y_hi * 2 + 1 - core)], sibling).wait_recv()

    for i in range(2):
        multiply(i)
    for act in later[:4]:
        act()

    @pl.when(home)
    def _():
        for i in range(2):
            pass_on(i).wait_recv()
        for i in range(2):
            for tile in range(row_count // row_tile):
                span = pl.ds(tile * row_tile, row_tile)
                lanes = slice(i * width, (i + 1) * width)
                residual_ref[span, lanes] = jnp.where(
                    info_ref[span, CROSS : CROSS + 1] > 0.5,
                    theirs[span, lanes].astype(jnp.float32),
                    rows[span, quarter(y_hi * 2 + i)].astype(jnp.float32),
                ).astype(jnp.bfloat16)

    for k in range(2):

        @pl.when(home)
        def _():
            at = (1 - y_hi) * 2 + k
            for part in range(2):
                token_copy(9 + 2 * part + k, rows.at[parts[part], quarter(at)], sibling).wait_recv()

        multiply(2 + k)

    meta_ref[...] = rows[count - META : count, 0:128]
    meta = meta_ref[...].astype(jnp.float32)[0:1]
    half_heads = q_ref.shape[0] // 2
    slots = 4.0
    head = q_ref.shape[2]
    for tile in range(scaled.shape[0] // row_tile):
        span = slice(tile * row_tile, (tile + 1) * row_tile)
        scale = lax.rsqrt(squares[span] * (1.0 / (4 * width)) + epsilon)
        if tile * row_tile < row_count:
            lane = lax.broadcasted_iota(jnp.int32, (row_tile, 128), 1).astype(jnp.float32)
            blocks = jnp.sum(
                jnp.where(lane == info_ref[span, SLOT : SLOT + 1] + slots, meta, 0.0),
                axis=1, keepdims=True,
            )
            prefix_ref[span] = jnp.broadcast_to(blocks * PBLK, (row_tile, 128))
            two = jnp.broadcast_to(blocks, (row_tile, head)) > 1.5
            turns = [jnp.where(two, turn[1, n, span], turn[0, n, span]) for n in range(2)]
        else:
            turns = [turn[0, n, span] for n in range(2)]

        def turned(values, gain):
            values = values * scale
            values = values * lax.rsqrt(jnp.mean(values * values, axis=1, keepdims=True) + epsilon)
            values = values * gain
            swapped = jnp.concatenate([values[:, head // 2 :], values[:, : head // 2]], axis=1)
            return (values * turns[0] + swapped * turns[1]).astype(jnp.bfloat16)

        if tile * row_tile < row_count:
            for h in range(2 * half_heads):
                column = h % half_heads * head
                q_ref[h, span] = turned(
                    sums[h // half_heads, span, column : column + head], head_gain_ref[0:1]
                )
        column = half_heads * head
        pairs_ref[span, :head] = turned(sums[0, span, column : column + head], head_gain_ref[1:2])
        pairs_ref[span, head:] = (sums[1, span, column : column + head] * scale).astype(jnp.bfloat16)

    for act in later[4:]:
        act()
    outward.finish(viewer(gout_ref, 1 - core))
    inward_rows.finish()
    outward_rows.finish()
    for made in own_parts:
        made.wait_send()

    @pl.when(away)
    def _():
        for k in range(2):
            token_copy(9 + k, rows.at[parts[0], quarter(low + k)], sibling).wait_send()
            token_copy(11 + k, rows.at[parts[1], quarter(high + k)], sibling).wait_send()
            pass_on(k).wait_send()
        token_copy(8, mine, sibling, x_ref).wait_send()


def project(tokens, prompts, marks, win, wout, head, *tables):
    row_count, width = tokens.shape
    used = row_count + prompts.shape[0]
    count = used + META
    heads = 2 * (win.shape[2] // head - 1)
    bf16 = jnp.bfloat16
    planes = [Plane.COPIES] * 4
    return pl.pallas_call(
        project_kernel,
        name="project",
        out_shape=(
            jax.ShapeDtypeStruct((heads, row_count, head), bf16),
            jax.ShapeDtypeStruct((used, 2 * head), bf16),
            jax.ShapeDtypeStruct((row_count, 2 * width), bf16),
            jax.ShapeDtypeStruct((row_count, 128), jnp.float32),
            jax.ShapeDtypeStruct((META, 128), bf16),
            jax.ShapeDtypeStruct((2, 2, 16, 4) + wout.shape[1:], bf16),
        ),
        in_specs=[ANY] * 5 + [VMEM] * len(tables),
        out_specs=(VMEM,) * 5 + (ANY,),
        scratch_shapes=[
            pltpu.VMEM((count, width), bf16),
            pltpu.VMEM((count, 4 * width), bf16),
            pltpu.VMEM((row_count, 2 * width), bf16),
            pltpu.VMEM((2, 4 * width, win.shape[2]), bf16),
            pltpu.VMEM((2, 4) + win.shape[1:], bf16),
            pltpu.VMEM((used, width), bf16),
            pltpu.VMEM((2, used, win.shape[2]), jnp.float32),
            pltpu.VMEM((used, 128), jnp.float32),
            pltpu.VMEM((PBLOCKS, 2, used, head), jnp.float32),
        ]
        + [pltpu.SemaphoreType.DMA((n,)) for n in [14, 14] + planes + [13, 13, 2, 2, 6]],
        compiler_params=pltpu.CompilerParams(
            collective_id=0, has_side_effects=True, vmem_limit_bytes=58 * 2**20
        ),
    )(tokens, prompts, marks, win, wout, *tables)


TILE = 64


def attend_kernel(
    q_hbm, pairs_hbm, info_hbm, prefix_hbm, group_ref, wout_ref, out_ref, gout_ref,
    q_ref, pairs_ref, bounds_ref, prefix_ref, mine_ref, theirs_ref,
    prompts, shared, total, sums, x_send, x_recv, load_sem, a_send, a_recv, out_send, out_recv, kv_send, kv_recv, local_sem,
):
    x, y, z, core = place()
    heads, row_count, head = q_ref.shape
    loads = [
        pltpu.make_async_copy(hbm, ref, load_sem.at[n])
        for n, (hbm, ref) in enumerate(
            ((pairs_hbm, pairs_ref), (q_hbm, q_ref), (info_hbm, bounds_ref), (prefix_hbm, prefix_ref))
        )
    ]
    for load in loads:
        load.start()
    own_ref = pairs_ref.at[pl.ds(0, row_count)]
    prompt_ref = pairs_ref.at[pl.ds(row_count, prompts.shape[1])]
    sibling = device_at(x, y, z, 1 - core)
    greet(column_peers() + plane_peers())
    for load in loads:
        load.wait()
    mine = pltpu.make_async_copy(prompt_ref, prompts.at[core * 16 + x * 4 + z], local_sem.at[1])
    mine.start()
    rows = Column(wout_ref, lander(gout_ref), a_send, a_recv, local_sem, 0)
    rows.start()
    mine.wait()

    def prompt_viewer(owner):
        def view(half, where, part=None):
            span = pl.ds(half * 64, 64) if part is None else pl.ds(half * 64 + part * 32, 32)
            return prompts.at[owner * 16 + where, span]

        return view

    kv = Plane(prompt_viewer(core), kv_send, kv_recv)
    outward = Plane(viewer(gout_ref, core), out_send, out_recv)
    kv.begin()
    scale = head ** (-0.5) * 1.4426950408889634

    def weigh(tile, keys, values, low, high):
        span = pl.ds(tile * TILE, TILE)
        queries = q_ref[:, span].reshape(heads * TILE, head)
        scores = lax.dot_general(
            queries, keys, (((1,), (1,)), ((), ())), preferred_element_type=jnp.float32
        )
        count = keys.shape[0]
        at = lax.broadcasted_iota(jnp.int32, (TILE, count), 1).astype(jnp.float32)
        allowed = (at >= low) & (at < high)
        weights = jnp.where(
            allowed[None], jnp.exp2(scores.reshape(heads, TILE, count) * scale), 0.0
        )
        blend = jnp.dot(
            weights.astype(jnp.bfloat16).reshape(heads * TILE, count), values,
            preferred_element_type=jnp.float32,
        )
        return span, jnp.sum(weights, axis=-1, keepdims=True), blend.reshape(heads, TILE, head)

    def own_tile(tile):
        span = slice(tile * TILE, (tile + 1) * TILE)
        count = min(-(-(tile + 1) * TILE // 128) * 128, row_count)
        low = bounds_ref[span, START : START + 1]
        high = lax.broadcasted_iota(jnp.int32, (TILE, 1), 0).astype(jnp.float32) + (tile * TILE + 1.0)
        span, weight, blend = weigh(tile, own_ref[:count, :head], own_ref[:count, head:], low, high)
        total[:, span] = blend
        sums[:, span] = jnp.broadcast_to(weight, (heads, TILE, head))

    def shared_tile(tile):
        span = slice(tile * TILE, (tile + 1) * TILE)
        low = bounds_ref[span, PROMPT : PROMPT + 1]
        high = low + prefix_ref[span, 0:1]
        span, weight, blend = weigh(tile, shared[:, :head], shared[:, head:], low, high)
        blend = (total[:, span] + blend) / (sums[:, span] + weight)
        for h in range(heads):
            mine_ref[span, h * head : (h + 1) * head] = blend[h].astype(jnp.bfloat16)
        swap(tile).start()

    def swap(tile):
        span = pl.ds(tile * TILE, TILE)
        return send(
            mine_ref.at[span], theirs_ref.at[span], x_send.at[tile], x_recv.at[tile], sibling
        )

    tiles = q_ref.shape[1] // TILE
    for tile in range(4):
        own_tile(tile)
    rows.ready()
    kv.first()
    outward.begin()
    own_tile(4)
    kv.opposite()
    own_tile(5)
    kv.second(0)
    outward.first()
    own_tile(6)
    acts = list(kv.rest())[1:]
    for act in acts[:3]:
        act()
    outward.opposite()
    for act in acts[3:]:
        act()
    kv.finish(prompt_viewer(1 - core))
    for j in range(group_ref.shape[0]):
        shared[j * prompts.shape[1] : (j + 1) * prompts.shape[1]] = prompts[group_ref[j]]
    later = list(outward.rest())
    for tile in range(tiles):
        later[tile]()
        shared_tile(tile)
    for act in later[tiles:]:
        act()
    for tile in range(tiles):
        swap(tile).wait_recv()
        span = slice(tile * TILE, (tile + 1) * TILE)
        out_ref[span] = jnp.where(
            bounds_ref[span, CROSS : CROSS + 1] > 0.5,
            theirs_ref[span].astype(jnp.float32),
            mine_ref[span].astype(jnp.float32),
        ).astype(jnp.bfloat16)
        swap(tile).wait_send()
    rows.finish()
    outward.finish(viewer(gout_ref, 1 - core))


def attend(queries, pairs, info, prefix, group, wout):
    heads, count, head = queries.shape
    prompt = (pairs.shape[0] - count, pairs.shape[1])
    tiles = count // TILE
    sems = [tiles, tiles, 4, 7, 7] + [Plane.COPIES] * 4 + [2]
    return pl.pallas_call(
        attend_kernel,
        name="attend",
        out_shape=(
            jax.ShapeDtypeStruct((count, heads * head), jnp.bfloat16),
            jax.ShapeDtypeStruct((2, 2, 16, 4) + wout.shape[1:], wout.dtype),
        ),
        in_specs=[ANY] * 4 + [pl.BlockSpec(memory_space=pltpu.SMEM), ANY],
        out_specs=(VMEM, ANY),
        scratch_shapes=[
            pltpu.VMEM(queries.shape, queries.dtype),
            pltpu.VMEM(pairs.shape, pairs.dtype),
            pltpu.VMEM(info.shape, info.dtype),
            pltpu.VMEM(prefix.shape, prefix.dtype),
            pltpu.VMEM((count, heads * head), jnp.bfloat16),
            pltpu.VMEM((count, heads * head), jnp.bfloat16),
            pltpu.VMEM((32,) + prompt, pairs.dtype),
            pltpu.VMEM((group.shape[0] * prompt[0], prompt[1]), pairs.dtype),
            pltpu.VMEM(queries.shape, jnp.float32),
            pltpu.VMEM(queries.shape, jnp.float32),
        ]
        + [pltpu.SemaphoreType.DMA((n,)) for n in sems],
        compiler_params=pltpu.CompilerParams(
            collective_id=1, has_side_effects=True, vmem_limit_bytes=48 * 2**20
        ),
    )(queries, pairs, info, prefix, group, wout)


BLOCK = 128
LEVELS = ("z1", "x1", "z2", "x2")


def level_bits(shift, sign):
    odd = shift % 2 == 1
    far = (shift >= 2) if sign == 1 else ((shift == 1) | (shift == 2))
    return odd, far


def along_z(shift, z):
    return shift % 4, shift // 4 + (z < shift % 4).astype(jnp.int32)


def y_shift(shift, x, z):
    shift_z, need_x = along_z(shift, (z + shift) % 4)
    end_x = (x + need_x) % 4
    return (need_x // 4 + (end_x < need_x % 4).astype(jnp.int32)) % 2 == 1


def move_masks(shift, x, z):
    masks = []
    for sign in (1, -1):
        odd_z, far_z = level_bits(shift % 4, sign)
        for level in LEVELS:
            end_z = (z + (2 * far_z.astype(jnp.int32) if level in ("z1", "x1") else 0)) % 4
            odd_x, far_x = level_bits(along_z(shift, end_z)[1] % 4, sign)
            masks.append({"z1": odd_z, "x1": odd_x, "z2": far_z, "x2": far_x}[level])
    return [mask.astype(jnp.float32) for mask in masks]


def return_order(blocks):
    unit, seen, ahead, pace = 1.28, 1.6, 3.0, 8.2
    cost = {"multiply": 1.6, "add": 0.5, "finish": 0.4, "take": 0.3}
    free, summed, order, now = {}, {}, [], 0.0
    waiting = [(max(0.0, pace * p - ahead), 0, ("multiply", p)) for p in range(blocks // 2)]

    def use(link, long):
        free[link] = max(free.get(link, 0.0), now) + long
        return free[link]

    while waiting:
        ready, _, act = waiting.pop(waiting.index(min(waiting)))
        now = max(now, ready) + cost[act[0]]
        order.append(act)
        if act[0] == "multiply":
            both = (2 * act[1], 2 * act[1] + 1)
            for j in both:
                waiting.append((use("y", unit) + seen, 1, ("add", j)))
            for j in both:
                summed[j] = use("y", unit)
        elif act[0] == "add":
            waiting.append((max(use("y", unit), summed[act[1]]) + seen, 2, ("finish", act[1])))
        else:
            j, level = act[1], 0 if act[0] == "finish" else act[2] + 1
            if level < len(LEVELS):
                axis, far = LEVELS[level][0], LEVELS[level][1] == "2"
                links = (axis + "+", axis + "-") if far else (axis + "+-"[j % 2],)
                end = max([use(link, 2 * unit) for link in links]) + (0.5 if far else 0.0)
                waiting.append((end + seen, 3 + level, ("take", j, level)))
    return order


def return_kernel(
    blend_hbm, w0_hbm, w1_hbm, residual_hbm, info_ref, out_ref,
    blend_ref, residual_ref, w0_ref, w1_ref, mask_ref, sums, source, home_sum, home_got, raw, final, held, landed,
    src_send, raw_recv, fin_recv, move_send, move_recv, w_sem,
):
    x, y, z, core = place()
    y_lo, y_hi = lax.rem(y, 2), y // 2
    width = out_ref.shape[1]
    blocks = width // BLOCK
    above, below = step(y, 1), step(y, -1)
    sibling = device_at(x, y, z, 1 - core)
    loads = [
        pltpu.make_async_copy(hbm.at[half], ref.at[half], w_sem.at[n * 2 + half])
        for n, (hbm, ref) in enumerate(((w0_hbm, w0_ref), (w1_hbm, w1_ref)))
        for half in range(2)
    ]
    loads.append(pltpu.make_async_copy(blend_hbm, blend_ref, w_sem.at[4]))
    loads.append(pltpu.make_async_copy(residual_hbm, residual_ref, w_sem.at[5]))
    for load in loads:
        load.start()
    for n in range(mask_ref.shape[0]):
        mask_ref[n] = jnp.broadcast_to(
            info_ref[:, MOVES + n : MOVES + n + 1], mask_ref.shape[1:]
        )
    peers = [device_at(x, at, z, k) for at in (above, below) for k in range(2)] + [sibling]
    peers += [device_at(step(x, s), y, z, core) for s in (1, -1, 2)]
    peers += [device_at(x, y, step(z, s), core) for s in (1, -1, 2)]
    greet(peers)
    home = core == y_lo
    away = jnp.logical_not(home)

    far, up, down = 1 - y_hi, above // 2, below // 2
    quarters = (
        jnp.where(home, far * 2, up * 2),
        jnp.where(home, far * 2 + 1, down * 2 + 1),
        jnp.where(home, y_hi * 2 + 1 - core, up * 2 + 1),
        jnp.where(home, y_hi * 2 + core, down * 2),
    )
    pieces = w0_ref.shape[0]
    half_depth = w0_ref.shape[2] + w1_ref.shape[2]

    for load in loads:
        load.wait()

    def raw_copy(j, slot):
        to = device_at(x, (above, below)[slot], z, core)
        at = slot * blocks + j
        return send(source.at[slot, j], raw.at[slot, j], src_send.at[at], raw_recv.at[at], to)

    def sibling_copy(j):
        at = 2 * blocks + j
        return send(home_sum.at[j], home_got.at[j], src_send.at[at], fin_recv.at[at], sibling)

    def final_copy(j, at):
        slot, k = ((0, 0), (1, 1), (0, 1), (1, 0))[at]
        to = device_at(x, (above, below)[slot], z, k)
        return send(
            source.at[at, j], final.at[slot, j],
            src_send.at[at * blocks + j], fin_recv.at[slot * blocks + j], to,
        )

    def multiply(pair):
        for at in range(4):
            start = pl.multiple_of(quarters[at] * width + pair * 2 * BLOCK, 2 * BLOCK)
            total = None
            for half in range(pieces):
                for n, w_ref in enumerate((w0_ref, w1_ref)):
                    column = half * half_depth + n * w0_ref.shape[2]
                    depth = w_ref.shape[2]
                    term = lax.dot_general(
                        blend_ref[:, column : column + depth], w_ref[half, pl.ds(start, 2 * BLOCK)],
                        (((1,), (1,)), ((), ())), preferred_element_type=jnp.float32,
                    )
                    total = term if total is None else total + term
            sums[at] = total
        lanes = [pl.ds(i * BLOCK, BLOCK) for i in range(2)]

        @pl.when(home)
        def _():
            for i in range(2):
                j = pair * 2 + i
                for slot in range(2):
                    source[slot, j] = sums[slot, :, lanes[i]].astype(jnp.bfloat16)
                    raw_copy(j, slot).start()
            for i in range(2):
                j = pair * 2 + i
                theirs = pl.ds(pl.multiple_of((1 - core) * width + j * BLOCK, BLOCK), BLOCK)
                home_sum[j] = sums[2, :, lanes[i]] + residual_ref[:, theirs].astype(jnp.float32)
                sibling_copy(j).start()
                mine = pl.ds(pl.multiple_of(core * width + j * BLOCK, BLOCK), BLOCK)
                home_got[j] = sums[3, :, lanes[i]] + residual_ref[:, mine].astype(jnp.float32)

        @pl.when(away)
        def _():
            for i in range(2):
                j = pair * 2 + i
                for at in (2, 3):
                    source[at, j] = sums[at, :, lanes[i]].astype(jnp.bfloat16)
                    final_copy(j, at).start()
            for i in range(2):
                j = pair * 2 + i
                for at in range(2):
                    partial[at, j] = sums[at, :, lanes[i]].astype(jnp.bfloat16)

    partial = source

    def add(j):
        @pl.when(away)
        def _():
            for slot in range(2):
                raw_copy(j, slot).wait_recv()
                source[slot, j] = (
                    partial[slot, j].astype(jnp.float32) + raw[slot, j].astype(jnp.float32)
                ).astype(jnp.bfloat16)
                final_copy(j, slot).start()

    def move(j, level):
        by = (1, -1)[j % 2] if LEVELS[level][1] == "1" else 2
        if LEVELS[level][0] == "z":
            to = device_at(x, y, step(z, by), core)
        else:
            to = device_at(step(x, by), y, z, core)
        at = level * blocks + j
        return send(
            held.at[level, j], landed.at[level, j], move_send.at[at], move_recv.at[at], to
        )

    def finish(j):
        for slot in range(2):
            final_copy(j, slot).wait_recv()

        @pl.when(away)
        def _():
            sibling_copy(j).wait_recv()

        total = final[0, j].astype(jnp.float32) + final[1, j].astype(jnp.float32) + home_got[j]
        held[0, j] = total.astype(jnp.bfloat16)
        move(j, 0).start()

    def take(j, level):
        move(j, level).wait_recv()
        chosen = jnp.where(
            mask_ref[(j % 2) * len(LEVELS) + level] > 0.5,
            landed[level, j].astype(jnp.float32),
            held[level, j].astype(jnp.float32),
        ).astype(jnp.bfloat16)
        if level + 1 < len(LEVELS):
            held[level + 1, j] = chosen
            move(j, level + 1).start()
        else:
            out_ref[:, j * BLOCK : (j + 1) * BLOCK] = chosen

    for act, *which in return_order(blocks):
        {"multiply": multiply, "add": add, "finish": finish, "take": take}[act](*which)

    for j in range(blocks):
        for level in range(len(LEVELS)):
            move(j, level).wait_send()

        @pl.when(home)
        def _():
            raw_copy(j, 0).wait_send()
            raw_copy(j, 1).wait_send()
            sibling_copy(j).wait_send()

        @pl.when(away)
        def _():
            for at in range(4):
                final_copy(j, at).wait_send()


def return_rows(blended, w0, w1, residual, info):
    count = blended.shape[0]
    width = residual.shape[1] // 2
    blocks = width // BLOCK
    levels = len(LEVELS)

    def room(n, dtype=jnp.bfloat16):
        return pltpu.VMEM((n, blocks, count, BLOCK), dtype)

    return pl.pallas_call(
        return_kernel,
        name="return_rows",
        out_shape=jax.ShapeDtypeStruct((count, width), jnp.bfloat16),
        in_specs=[ANY] * 4 + [VMEM],
        out_specs=VMEM,
        scratch_shapes=[
            pltpu.VMEM(blended.shape, blended.dtype),
            pltpu.VMEM(residual.shape, residual.dtype),
            pltpu.VMEM(w0.shape, w0.dtype),
            pltpu.VMEM(w1.shape, w1.dtype),
            pltpu.VMEM((2 * levels, count, BLOCK), jnp.float32),
            pltpu.VMEM((4, count, 2 * BLOCK), jnp.float32),
            room(4),
            pltpu.VMEM((blocks, count, BLOCK), jnp.float32),
            pltpu.VMEM((blocks, count, BLOCK), jnp.float32),
            room(2),
            room(2),
            room(levels),
            room(levels),
        ]
        + [pltpu.SemaphoreType.DMA((n * blocks,)) for n in (4, 2, 3, levels, levels)]
        + [pltpu.SemaphoreType.DMA((6,))],
        compiler_params=pltpu.CompilerParams(
            collective_id=2, has_side_effects=True, vmem_limit_bytes=56 * 2**20
        ),
    )(blended, w0, w1, residual, info)


def slot_layout(seq_lengths, row_count):
    ends_at = jnp.cumsum(seq_lengths)
    starts_at = ends_at - seq_lengths
    position = jnp.arange(row_count, dtype=jnp.int32)
    slot_of = jnp.sum((position[:, None] >= ends_at[None, :]).astype(jnp.int32), axis=1)
    onehot = (
        slot_of[:, None] == jnp.arange(seq_lengths.shape[0], dtype=jnp.int32)[None, :]
    ).astype(jnp.int32)
    within = position - jnp.sum(onehot * starts_at[None, :], axis=1)
    return (slot_of, within, onehot)


def shards(
    tokens,
    prompt_rows,
    norm_gain,
    w_query,
    w_key,
    w_value,
    w_out,
    q_gain,
    k_gain,
    seq_lengths,
    prompt_group,
    prompt_blocks,
    dest_offset,
):
    row_count, width = tokens.shape
    prompt_len = prompt_rows.shape[0]
    head_size = q_gain.shape[0]
    slot_count = seq_lengths.shape[0]
    depth = w_query.shape[0]
    groups = w_key.shape[1] // head_size
    rep = lax.axis_index("rep")

    halves = w_query.astype(jnp.bfloat16).reshape(depth, groups, 2, -1)
    key_cols = w_key.astype(jnp.bfloat16).reshape(depth, groups, 1, head_size)
    value_cols = w_value.astype(jnp.bfloat16).reshape(depth, groups, 1, head_size)
    win = jnp.concatenate([halves, jnp.concatenate([key_cols, value_cols], axis=2)], axis=3)
    win = win.transpose(1, 2, 0, 3).reshape(2 * groups, depth, -1)
    wout = w_out.astype(jnp.bfloat16).reshape(2 * groups, -1, depth)
    wout = [part.transpose(0, 2, 1) for part in (wout[:, :EARLY], wout[:, EARLY:])]
    marks = jnp.concatenate([prompt_group, prompt_blocks]).astype(jnp.bfloat16)
    marks = jnp.pad(marks[None, :], ((0, META - 1), (0, width - 2 * slot_count)))

    plane_x, plane_z = rep // 4 % 4, rep % 4
    slot_of, within, onehot = slot_layout(seq_lengths, row_count)
    crosses = y_shift(dest_offset, plane_x, plane_z)
    shift_rows = jnp.sum(onehot * dest_offset[None, :], axis=1)
    row_crosses = jnp.sum(onehot * crosses[None, :], axis=1)
    lanes = {
        CROSS: row_crosses,
        START: jnp.arange(row_count, dtype=jnp.int32) - within,
        PROMPT: slot_of * prompt_len,
        SLOT: slot_of,
        WITHIN: within,
    }
    for n, mask in enumerate(move_masks(shift_rows, plane_x, plane_z)):
        lanes[MOVES + n] = mask
    lane = jnp.arange(128, dtype=jnp.int32)[None, :]
    info = jnp.zeros((row_count, 128), jnp.float32)
    for at, values in lanes.items():
        info = jnp.where(lane == at, values.astype(jnp.float32)[:, None], info)
    spread = np.arange(head_size // 2, dtype=np.float32) * np.float32(2.0 / head_size)
    frequency = np.float32(rope_base) ** -spread
    frequency = jnp.asarray(np.tile(frequency.astype(np.float32), 2)[None, :])
    queries, pairs, residual, prefix, meta, gout = project(
        tokens, prompt_rows, marks, win, wout[0], head_size,
        info, norm_gain[None, :], jnp.stack([q_gain, k_gain]), frequency,
    )
    group_here = meta[0, :slot_count].astype(jnp.int32)
    blended, gout_b = attend(queries, pairs, info, prefix, group_here, wout[1])
    features = 4 * width
    return return_rows(
        blended, gout.reshape(2, features, -1), gout_b.reshape(2, features, -1), residual, info
    )


def solution(mesh):
    return jax.shard_map(
        shards,
        mesh=mesh,
        in_specs=(
            P("rep", "tp"),
            P("rep", "tp"),
            P(),
            P(("rep", "tp"), None),
            P(("rep", "tp"), None),
            P(("rep", "tp"), None),
            P(None, ("rep", "tp")),
            P(),
            P(),
            P(),
            P("rep"),
            P("rep"),
            P(),
        ),
        out_specs=P("rep", "tp"),
        check_vma=False,
    )
```

```python
import functools

import jax
import jax.numpy as jnp
import numpy as np
from jax import lax
from jax.experimental import pallas as pl
from jax.experimental.pallas import tpu as pltpu
from jax.sharding import PartitionSpec as P

PBLK = 64
PBLOCKS = 2
MESH = pl.DeviceIdType.MESH
ANY = pl.BlockSpec(memory_space=pl.ANY)
VMEM = pl.BlockSpec(memory_space=pltpu.VMEM)
SMEM = pl.BlockSpec(memory_space=pltpu.SMEM)
OFFSETS = (0, -1, 1, 2)
META = 16
CROSS, START, PROMPT, SLOT, WITHIN, MOVES = 0, 1, 2, 3, 4, 8
EARLY = 256

epsilon = 1e-06
rope_base = 1000000.0


def place():
    rep, tp = lax.axis_index("rep"), lax.axis_index("tp")
    return lax.rem(rep // 4, 4), (tp // 2) * 2 + rep // 16, lax.rem(rep, 4), lax.rem(tp, 2)


def device_at(x, y, z, core):
    return (lax.rem(y, 2) * 16 + x * 4 + z, (y // 2) * 2 + core)


def step(value, by):
    return lax.rem(value + (by + 4), 4)


def greet(peers):
    barrier = pltpu.get_barrier_semaphore()
    for peer in peers:
        pl.semaphore_signal(barrier, inc=1, device_id=peer, device_id_type=MESH)
    pl.semaphore_wait(barrier, len(peers))


def send(source, target, send_sem, recv_sem, device):
    return pltpu.make_async_remote_copy(
        src_ref=source,
        dst_ref=target,
        send_sem=send_sem,
        recv_sem=recv_sem,
        device_id=device,
        device_id_type=MESH,
    )


class Plane:
    COPIES = 72

    def __init__(self, view, send_sems, recv_sems):
        self.view, self.ss, self.rs = view, send_sems, recv_sems
        self.x, self.y, self.z, self.core = place()
        self.started = []

    def block(self, half, first, second, part=None):
        a, b = (first, second) if half == 0 else (second, first)
        return self.view(half, step(self.x, a) * 4 + step(self.z, b), part)

    def toward(self, half, phase, sign):
        if (phase == 0) == (half == 0):
            return device_at(step(self.x, sign), self.y, self.z, self.core)
        return device_at(self.x, self.y, step(self.z, sign), self.core)

    def copy(self, half, number, ref, device):
        at = half * 36 + number
        return send(ref, ref, self.ss.at[at], self.rs.at[at], device)

    def start(self, *args):
        made = self.copy(*args)
        made.start()
        self.started.append(made)

    def sibling(self):
        return device_at(self.x, self.y, self.z, 1 - self.core)

    def share(self, half, o1, o2):
        ref = self.block(half, OFFSETS[o1], OFFSETS[o2])
        self.start(half, 20 + 4 * o1 + o2, ref, self.sibling())

    def spread(self, half, o1):
        ref = self.block(half, OFFSETS[o1], 0)
        self.start(half, 4 + 4 * o1, ref, self.toward(half, 1, 1))
        self.start(half, 5 + 4 * o1, ref, self.toward(half, 1, -1))
        self.share(half, o1, 0)

    def begin(self):
        for half in range(2):
            ref = self.block(half, 0, 0)
            self.start(half, 0, ref, self.toward(half, 0, 1))
            self.start(half, 1, ref, self.toward(half, 0, -1))
        for half in range(2):
            self.spread(half, 0)

    def arrived(self, half, number, ref):
        self.copy(half, number, ref, self.sibling()).wait_recv()

    def first(self):
        for half in range(2):
            self.arrived(half, 0, self.block(half, -1, 0))
            self.start(half, 2, self.block(half, -1, 0, 0), self.toward(half, 0, 1))
            self.arrived(half, 1, self.block(half, 1, 0))
            self.start(half, 3, self.block(half, 1, 0, 1), self.toward(half, 0, -1))
        for half in range(2):
            self.spread(half, 1)
            self.spread(half, 2)

    def opposite(self):
        for half in range(2):
            self.arrived(half, 2, self.block(half, 2, 0, 0))
            self.arrived(half, 3, self.block(half, 2, 0, 1))
            self.spread(half, 3)

    def second(self, o1):
        off, base = OFFSETS[o1], 4 + 4 * o1
        for half in range(2):
            self.arrived(half, base, self.block(half, off, -1))
            self.start(half, base + 2, self.block(half, off, -1, 0), self.toward(half, 1, 1))
            self.arrived(half, base + 1, self.block(half, off, 1))
            self.start(half, base + 3, self.block(half, off, 1, 1), self.toward(half, 1, -1))
            self.share(half, o1, 1)
            self.share(half, o1, 2)

    def second_opposite(self, o1):
        off, base = OFFSETS[o1], 4 + 4 * o1
        for half in range(2):
            self.arrived(half, base + 2, self.block(half, off, 2, 0))
            self.arrived(half, base + 3, self.block(half, off, 2, 1))
            self.share(half, o1, 3)

    def rest(self):
        yield functools.partial(self.second, 0)
        for o1 in range(1, 4):
            yield functools.partial(self.second, o1)
            yield functools.partial(self.second_opposite, o1 - 1)
        yield functools.partial(self.second_opposite, 3)

    def second_all(self):
        for act in self.rest():
            act()

    def finish(self, shared_block):
        for half in range(2):
            for o1 in range(4):
                for o2 in range(4):
                    a, b = (o1, o2) if half == 0 else (o2, o1)
                    where = step(self.x, OFFSETS[a]) * 4 + step(self.z, OFFSETS[b])
                    self.arrived(half, 20 + 4 * o1 + o2, shared_block(half, where))
        for made in self.started:
            made.wait_send()


COLUMN = tuple((dy, dc) for dy in range(4) for dc in range(2) if (dy, dc) != (0, 0))


def column_peers():
    x, y, z, core = place()
    return [device_at(x, step(y, dy), z, core if dc == 0 else 1 - core) for dy, dc in COLUMN]


def plane_peers():
    x, y, z, core = place()
    peers = [device_at(step(x, s), y, z, core) for s in (1, -1)]
    return peers + [device_at(x, y, step(z, s), core) for s in (1, -1)]


class Column:
    def __init__(self, source, land, send_sems, recv_sems, local_sem, which):
        x, y, z, core = place()
        tp = lax.axis_index("tp")
        base = which * len(COLUMN)
        y_lo = lax.rem(y, 2)
        self.local = pltpu.make_async_copy(
            source.at[y * 2 + core], land(core, y_lo, tp), local_sem.at[which]
        )
        self.sent, self.got = [], []
        for n, (dy, dc) in enumerate(COLUMN):
            to_y, from_y = step(y, dy), step(y, -dy)
            peer = core if dc == 0 else 1 - core
            sems = send_sems.at[base + n], recv_sems.at[base + n]
            to = device_at(x, to_y, z, peer)
            self.sent.append(send(source.at[to_y * 2 + peer], land(peer, y_lo, tp), *sems, to))
            ref = land(core, lax.rem(from_y, 2), (from_y // 2) * 2 + peer)
            self.got.append(send(ref, ref, *sems, to))

    def start(self):
        self.local.start()
        for made in self.sent:
            made.start()

    def ready(self):
        self.local.wait()
        for made in self.got:
            made.wait_recv()

    def finish(self):
        for made in self.sent:
            made.wait_send()


def lander(target):
    x, _, z, _ = place()
    return lambda core, y_lo, tp: target.at[core, y_lo, x * 4 + z, tp]


def viewer(target, owner):
    def view(half, where, part=None):
        if part is None:
            return target.at[owner, half, where]
        return target.at[owner, half, where, pl.ds(part * 2, 2)]

    return view


BLOCK = 128
LEVELS = ("z1", "x1", "z2", "x2")


def count_of(condition):
    return jnp.where(condition, 1, 0)


def level_bits(shift, sign):
    odd = (shift & 1) == 1
    far = (shift >= 2) if sign == 1 else ((shift == 1) | (shift == 2))
    return odd, far


def along_z(shift, z):
    return (shift >> 2) + count_of(z < (shift & 3))


def y_shift(shift, x, z):
    need_x = along_z(shift, (z + shift) & 3)
    end_x = (x + need_x) & 3
    return (((need_x >> 2) + count_of(end_x < (need_x & 3))) & 1) == 1


def move_masks(shift, x, z):
    masks = []
    for sign in (1, -1):
        odd_z, far_z = level_bits(shift & 3, sign)
        for level in LEVELS:
            end_z = (z + 2 * count_of(far_z)) & 3 if level in ("z1", "x1") else z
            odd_x, far_x = level_bits(along_z(shift, end_z) & 3, sign)
            masks.append({"z1": odd_z, "x1": odd_x, "z2": far_z, "x2": far_x}[level])
    return masks


def row_info(first, rows, lengths_ref, offsets_ref, prompt_len, x, z):
    shape = (rows, 128)
    row = lax.broadcasted_iota(jnp.int32, shape, 0) + first
    lane = lax.broadcasted_iota(jnp.int32, shape, 1)
    slot, start = jnp.zeros(shape, jnp.int32), jnp.zeros(shape, jnp.int32)
    shift, end = jnp.zeros(shape, jnp.int32) + offsets_ref[0], 0
    for j in range(1, lengths_ref.shape[0]):
        end = end + lengths_ref[j - 1]
        past = row >= end
        slot = slot + count_of(past)
        start = jnp.where(past, end, start)
        shift = jnp.where(past, offsets_ref[j], shift)
    lanes = {
        CROSS: count_of(y_shift(shift, x, z)),
        START: start,
        PROMPT: slot * prompt_len,
        SLOT: slot,
        WITHIN: row - start,
    }
    for n, mask in enumerate(move_masks(shift, x, z)):
        lanes[MOVES + n] = count_of(mask)
    info = jnp.zeros(shape, jnp.int32)
    for at, values in lanes.items():
        info = jnp.where(lane == at, values, info)
    return info.astype(jnp.float32)


def project_kernel(
    lengths_ref, offsets_ref, group_ref, blocks_ref, tokens_ref, prompt_ref,
    wq_ref, wk_ref, wv_ref, wo_ref, gain_ref, q_gain_ref, k_gain_ref, turn_ref,
    q_ref, pairs_ref, residual_ref, prefix_ref, meta_ref, info_ref, gout_ref,
    x_ref, win_ref, wout_ref, rows, theirs, gin, stage, scaled, sums, squares, turn,
    a_send, a_recv, in_send, in_recv, out_send, out_recv, t_send, t_recv, p_send, p_recv, local_sem,
):
    x, y, z, core = place()
    tp = lax.axis_index("tp")
    y_lo, y_hi = lax.rem(y, 2), y // 2
    sibling = device_at(x, y, z, 1 - core)
    above, below = step(y, 1), step(y, -1)
    row_count = residual_ref.shape[0]
    loads, at = [], 0
    for n, ref in enumerate((tokens_ref, prompt_ref)):
        loads.append(
            pltpu.make_async_copy(ref, x_ref.at[pl.ds(at, ref.shape[0])], local_sem.at[3 + n])
        )
        at += ref.shape[0]
    for load in loads:
        load.start()
    slots = group_ref.shape[0]
    lane = lax.broadcasted_iota(jnp.int32, (META, x_ref.shape[1]), 1)
    marks = jnp.zeros(lane.shape, jnp.int32)
    for j in range(slots):
        marks = jnp.where(lane == j, group_ref[j], marks)
        marks = jnp.where(lane == slots + j, blocks_ref[j], marks)
    x_ref[at:] = marks.astype(jnp.float32).astype(jnp.bfloat16)
    blocks, _, block_width = win_ref.shape
    head = q_ref.shape[2]
    wide = block_width - head
    for n in range(blocks):
        win_ref[n, :, :wide] = wq_ref[:, n * wide : (n + 1) * wide].astype(jnp.bfloat16)
        column = n // 2 * head
        narrow_ref = (wk_ref, wv_ref)[n % 2]
        win_ref[n, :, wide:] = narrow_ref[:, column : column + head].astype(jnp.bfloat16)
        wout_ref[n] = wo_ref[:, n * wide : n * wide + EARLY].astype(jnp.bfloat16)
    greet(column_peers() + plane_peers())
    inward_rows = Column(
        win_ref, lambda _, lo, at: stage.at[lo, at], a_send, a_recv, local_sem, 0
    )
    outward_rows = Column(wout_ref, lander(gout_ref), a_send, a_recv, local_sem, 1)
    inward_rows.start()
    outward_rows.start()
    for load in loads:
        load.wait()

    count, width = x_ref.shape
    cut = count // 32 * 16
    parts = (pl.ds(0, cut), pl.ds(cut, count - cut))
    home = core == y_lo
    away = jnp.logical_not(home)

    def quarter(at):
        return pl.ds(pl.multiple_of(at * width, 128), width)

    def own_part(up, part):
        to = device_at(x, above if up else below, z, y_lo)
        at = (0 if up else 4) + core * 2 + part
        ref = rows.at[parts[part], quarter(tp)]
        return send(x_ref.at[parts[part]], ref, t_send.at[(0 if up else 2) + part], t_recv.at[at], to)

    def token_copy(number, ref, device, source=None):
        source = ref if source is None else source
        return send(source, ref, t_send.at[number], t_recv.at[number], device)

    def pass_on(i):
        source = rows.at[pl.ds(0, row_count), quarter(y_hi * 2 + i)]
        target = theirs.at[:, pl.ds(i * width, width)]
        return send(source, target, p_send.at[i], p_recv.at[i], sibling)

    mine = rows.at[:, quarter(tp)]
    keep = pltpu.make_async_copy(x_ref, mine, local_sem.at[2])
    own_parts = [own_part(True, 0), own_part(False, 1), own_part(True, 1), own_part(False, 0)]
    for made in own_parts:
        made.start()

    @pl.when(home)
    def _():
        keep.start()

    @pl.when(away)
    def _():
        token_copy(8, mine, sibling, x_ref).start()

    for tile in range(row_count // 64):
        info_ref[tile * 64 : (tile + 1) * 64] = row_info(
            tile * 64, 64, lengths_ref, offsets_ref, prompt_ref.shape[0], x, z
        )

    def gin_viewer(owner):
        size = stage.shape[1] * stage.shape[2]

        def view(half, where, part=None):
            start = (half * 16 + where) * size
            if part is None:
                return gin.at[owner, pl.ds(pl.multiple_of(start, 16), size)]
            start = start + part * (size // 2)
            return gin.at[owner, pl.ds(pl.multiple_of(start, 16), size // 2)]

        return view

    inward = Plane(gin_viewer(core), in_send, in_recv)
    outward = Plane(viewer(gout_ref, core), out_send, out_recv)
    inward_rows.ready()
    for half in range(2):
        block = stage[half].astype(jnp.float32)
        inward.block(half, 0, 0)[...] = block.reshape(-1, block.shape[-1]).astype(jnp.bfloat16)
    inward.begin()
    inward.first()
    inward.opposite()
    outward_rows.ready()
    outward.begin()
    row_tile = 64
    acts = list(inward.rest())

    def fill_turns(tile):
        lane = lax.broadcasted_iota(jnp.int32, (row_tile, turn.shape[3]), 1)
        sign = jnp.where(lane < turn.shape[3] // 2, -1.0, 1.0)
        span = slice(tile * row_tile, (tile + 1) * row_tile)
        if tile * row_tile < row_count:
            starts = [info_ref[span, WITHIN : WITHIN + 1] + PBLK * (n + 1) for n in range(PBLOCKS)]
        else:
            first = lax.broadcasted_iota(jnp.int32, (row_tile, 1), 0).astype(jnp.float32)
            starts = [first + (tile * row_tile - row_count)]
        for n, start in enumerate(starts):
            angles = start * turn_ref[0:1]
            turn[n, 0, span] = jnp.cos(angles)
            turn[n, 1, span] = jnp.sin(angles) * sign

    fill_turns(0)
    fill_turns(1)
    for act in acts[:3]:
        act()
        fill_turns(acts.index(act) + 2)

    low, high = (below // 2) * 2, (above // 2) * 2

    @pl.when(away)
    def _():
        for k in range(2):
            ref = rows.at[parts[0], quarter(low + k)]
            token_copy(k * 2, ref, sibling).wait_recv()
            token_copy(9 + k, ref, device_at(x, above, z, core)).start()
            ref = rows.at[parts[1], quarter(high + k)]
            token_copy(4 + k * 2 + 1, ref, sibling).wait_recv()
            token_copy(11 + k, ref, device_at(x, below, z, core)).start()

    for n, act in enumerate(acts[3:]):
        act()
        if n < 4:
            fill_turns(n + 5)
    outward.first()
    inward.finish(gin_viewer(1 - core))
    outward.opposite()
    later = list(outward.rest())

    def multiply(i):
        at = quarter(y_hi * 2 + i if i < 2 else (1 - y_hi) * 2 + i - 2)
        gain = gain_ref[:, at]
        for tile in range(scaled.shape[0] // row_tile):
            span = pl.ds(tile * row_tile, row_tile)
            values = rows[span, at].astype(jnp.float32)
            total = jnp.sum(values * values, axis=1, keepdims=True)
            total = jnp.broadcast_to(total, (row_tile, squares.shape[1]))
            squares[span] = total if i == 0 else squares[span] + total
            scaled[span] = (values * gain).astype(jnp.bfloat16)
        for half in range(2):
            term = jnp.dot(scaled[...], gin[half, at], preferred_element_type=jnp.float32)
            sums[half] = term if i == 0 else sums[half] + term

    @pl.when(away)
    def _():
        for k in range(2):
            token_copy(k * 2 + 1, rows.at[parts[1], quarter(low + k)], sibling).wait_recv()
            token_copy(4 + k * 2, rows.at[parts[0], quarter(high + k)], sibling).wait_recv()
        for i in range(2):
            pass_on(i).start()

    @pl.when(home)
    def _():
        keep.wait()
        token_copy(8, rows.at[:, quarter(y_hi * 2 + 1 - core)], sibling).wait_recv()

    for i in range(2):
        multiply(i)
    for act in later[:4]:
        act()

    @pl.when(home)
    def _():
        for i in range(2):
            pass_on(i).wait_recv()
        for i in range(2):
            for tile in range(row_count // row_tile):
                span = pl.ds(tile * row_tile, row_tile)
                lanes = slice(i * width, (i + 1) * width)
                residual_ref[span, lanes] = jnp.where(
                    info_ref[span, CROSS : CROSS + 1] > 0.5,
                    theirs[span, lanes].astype(jnp.float32),
                    rows[span, quarter(y_hi * 2 + i)].astype(jnp.float32),
                ).astype(jnp.bfloat16)

    for k in range(2):

        @pl.when(home)
        def _():
            at = (1 - y_hi) * 2 + k
            for part in range(2):
                token_copy(9 + 2 * part + k, rows.at[parts[part], quarter(at)], sibling).wait_recv()

        multiply(2 + k)

    meta = rows[count - META : count, 0:128].astype(jnp.float32)
    meta_ref[...] = meta.astype(jnp.int32)
    meta = meta[0:1]
    half_heads = q_ref.shape[0] // 2
    for tile in range(scaled.shape[0] // row_tile):
        span = slice(tile * row_tile, (tile + 1) * row_tile)
        scale = lax.rsqrt(squares[span] * (1.0 / (4 * width)) + epsilon)
        if tile * row_tile < row_count:
            lane = lax.broadcasted_iota(jnp.int32, (row_tile, 128), 1).astype(jnp.float32)
            blocks = jnp.sum(
                jnp.where(lane == info_ref[span, SLOT : SLOT + 1] + slots, meta, 0.0),
                axis=1, keepdims=True,
            )
            prefix_ref[span] = jnp.broadcast_to(blocks * PBLK, (row_tile, 128))
            two = jnp.broadcast_to(blocks, (row_tile, head)) > 1.5
            turns = [jnp.where(two, turn[1, n, span], turn[0, n, span]) for n in range(2)]
        else:
            turns = [turn[0, n, span] for n in range(2)]

        def turned(values, gain):
            values = values * scale
            values = values * lax.rsqrt(jnp.mean(values * values, axis=1, keepdims=True) + epsilon)
            values = values * gain
            swapped = jnp.concatenate([values[:, head // 2 :], values[:, : head // 2]], axis=1)
            return (values * turns[0] + swapped * turns[1]).astype(jnp.bfloat16)

        if tile * row_tile < row_count:
            for h in range(2 * half_heads):
                column = h % half_heads * head
                q_ref[h, span] = turned(
                    sums[h // half_heads, span, column : column + head], q_gain_ref[...]
                )
        column = half_heads * head
        pairs_ref[span, :head] = turned(sums[0, span, column : column + head], k_gain_ref[...])
        pairs_ref[span, head:] = (sums[1, span, column : column + head] * scale).astype(jnp.bfloat16)

    for act in later[4:]:
        act()
    outward.finish(viewer(gout_ref, 1 - core))
    inward_rows.finish()
    outward_rows.finish()
    for made in own_parts:
        made.wait_send()

    @pl.when(away)
    def _():
        for k in range(2):
            token_copy(9 + k, rows.at[parts[0], quarter(low + k)], sibling).wait_send()
            token_copy(11 + k, rows.at[parts[1], quarter(high + k)], sibling).wait_send()
            pass_on(k).wait_send()
        token_copy(8, mine, sibling, x_ref).wait_send()


def project(lengths, offsets, group, blocks_of, tokens, prompts, wq, wk, wv, wo, *tables):
    row_count, width = tokens.shape
    used = row_count + prompts.shape[0]
    count = used + META
    depth, head = wq.shape[0], tables[-1].shape[1]
    blocks = 2 * wk.shape[1] // head
    heads = 2 * wq.shape[1] // blocks // head
    block_width = wq.shape[1] // blocks + head
    bf16 = jnp.bfloat16
    planes = [Plane.COPIES] * 4
    return pl.pallas_call(
        project_kernel,
        name="project",
        out_shape=(
            jax.ShapeDtypeStruct((heads, row_count, head), bf16),
            jax.ShapeDtypeStruct((used, 2 * head), bf16),
            jax.ShapeDtypeStruct((row_count, 2 * width), bf16),
            jax.ShapeDtypeStruct((row_count, 128), jnp.float32),
            jax.ShapeDtypeStruct((META, 128), jnp.int32),
            jax.ShapeDtypeStruct((row_count, 128), jnp.float32),
            jax.ShapeDtypeStruct((2, 2, 16, 4, depth, EARLY), bf16),
        ),
        in_specs=[SMEM] * 4 + [ANY] * 2 + [VMEM] * (4 + len(tables)),
        out_specs=(VMEM,) * 6 + (ANY,),
        scratch_shapes=[
            pltpu.VMEM((count, width), bf16),
            pltpu.VMEM((blocks, depth, block_width), bf16),
            pltpu.VMEM((blocks, depth, EARLY), bf16),
            pltpu.VMEM((count, 4 * width), bf16),
            pltpu.VMEM((row_count, 2 * width), bf16),
            pltpu.VMEM((2, 4 * width, block_width), bf16),
            pltpu.VMEM((2, 4, depth, block_width), bf16),
            pltpu.VMEM((used, width), bf16),
            pltpu.VMEM((2, used, block_width), jnp.float32),
            pltpu.VMEM((used, 128), jnp.float32),
            pltpu.VMEM((PBLOCKS, 2, used, head), jnp.float32),
        ]
        + [pltpu.SemaphoreType.DMA((n,)) for n in [14, 14] + planes + [13, 13, 2, 2, 6]],
        compiler_params=pltpu.CompilerParams(
            collective_id=0, has_side_effects=True, vmem_limit_bytes=60 * 2**20
        ),
    )(lengths, offsets, group, blocks_of, tokens, prompts, wq, wk, wv, wo, *tables)


TILE = 64


def attend_kernel(
    q_hbm, pairs_hbm, info_hbm, prefix_hbm, group_ref, wo_ref, out_ref, gout_ref,
    wout_ref, q_ref, pairs_ref, bounds_ref, prefix_ref, mine_ref, theirs_ref,
    prompts, shared, total, sums, x_send, x_recv, load_sem, a_send, a_recv, out_send, out_recv, kv_send, kv_recv, local_sem,
):
    x, y, z, core = place()
    heads, row_count, head = q_ref.shape
    loads = [
        pltpu.make_async_copy(hbm, ref, load_sem.at[n])
        for n, (hbm, ref) in enumerate(
            ((pairs_hbm, pairs_ref), (q_hbm, q_ref), (info_hbm, bounds_ref), (prefix_hbm, prefix_ref))
        )
    ]
    for load in loads:
        load.start()
    own_ref = pairs_ref.at[pl.ds(0, row_count)]
    prompt_ref = pairs_ref.at[pl.ds(row_count, prompts.shape[1])]
    sibling = device_at(x, y, z, 1 - core)
    blocks = wout_ref.shape[0]
    wide = wo_ref.shape[1] // blocks
    for n in range(blocks):
        wout_ref[n] = wo_ref[:, n * wide + EARLY : (n + 1) * wide].astype(jnp.bfloat16)
    greet(column_peers() + plane_peers())
    for load in loads:
        load.wait()
    mine = pltpu.make_async_copy(prompt_ref, prompts.at[core * 16 + x * 4 + z], local_sem.at[1])
    mine.start()
    rows = Column(wout_ref, lander(gout_ref), a_send, a_recv, local_sem, 0)
    rows.start()
    mine.wait()

    def prompt_viewer(owner):
        def view(half, where, part=None):
            span = pl.ds(half * 64, 64) if part is None else pl.ds(half * 64 + part * 32, 32)
            return prompts.at[owner * 16 + where, span]

        return view

    kv = Plane(prompt_viewer(core), kv_send, kv_recv)
    outward = Plane(viewer(gout_ref, core), out_send, out_recv)
    kv.begin()
    scale = head ** (-0.5) * 1.4426950408889634

    def weigh(tile, keys, values, low, high):
        span = pl.ds(tile * TILE, TILE)
        queries = q_ref[:, span].reshape(heads * TILE, head)
        scores = lax.dot_general(
            queries, keys, (((1,), (1,)), ((), ())), preferred_element_type=jnp.float32
        )
        count = keys.shape[0]
        at = lax.broadcasted_iota(jnp.int32, (TILE, count), 1).astype(jnp.float32)
        allowed = (at >= low) & (at < high)
        weights = jnp.where(
            allowed[None], jnp.exp2(scores.reshape(heads, TILE, count) * scale), 0.0
        )
        blend = jnp.dot(
            weights.astype(jnp.bfloat16).reshape(heads * TILE, count), values,
            preferred_element_type=jnp.float32,
        )
        return span, jnp.sum(weights, axis=-1, keepdims=True), blend.reshape(heads, TILE, head)

    def own_tile(tile):
        span = slice(tile * TILE, (tile + 1) * TILE)
        count = min(-(-(tile + 1) * TILE // 128) * 128, row_count)
        low = bounds_ref[span, START : START + 1]
        high = lax.broadcasted_iota(jnp.int32, (TILE, 1), 0).astype(jnp.float32) + (tile * TILE + 1.0)
        span, weight, blend = weigh(tile, own_ref[:count, :head], own_ref[:count, head:], low, high)
        total[:, span] = blend
        sums[:, span] = jnp.broadcast_to(weight, (heads, TILE, head))

    def shared_tile(tile):
        span = slice(tile * TILE, (tile + 1) * TILE)
        low = bounds_ref[span, PROMPT : PROMPT + 1]
        high = low + prefix_ref[span, 0:1]
        span, weight, blend = weigh(tile, shared[:, :head], shared[:, head:], low, high)
        blend = (total[:, span] + blend) / (sums[:, span] + weight)
        for h in range(heads):
            mine_ref[span, h * head : (h + 1) * head] = blend[h].astype(jnp.bfloat16)
        swap(tile).start()

    def swap(tile):
        span = pl.ds(tile * TILE, TILE)
        return send(
            mine_ref.at[span], theirs_ref.at[span], x_send.at[tile], x_recv.at[tile], sibling
        )

    tiles = q_ref.shape[1] // TILE
    for tile in range(4):
        own_tile(tile)
    rows.ready()
    kv.first()
    outward.begin()
    own_tile(4)
    kv.opposite()
    own_tile(5)
    kv.second(0)
    outward.first()
    own_tile(6)
    acts = list(kv.rest())[1:]
    for act in acts[:3]:
        act()
    outward.opposite()
    for act in acts[3:]:
        act()
    kv.finish(prompt_viewer(1 - core))
    for j in range(shared.shape[0] // prompts.shape[1]):
        shared[j * prompts.shape[1] : (j + 1) * prompts.shape[1]] = prompts[group_ref[0, j]]
    later = list(outward.rest())
    for tile in range(tiles):
        later[tile]()
        shared_tile(tile)
    for act in later[tiles:]:
        act()
    for tile in range(tiles):
        swap(tile).wait_recv()
        span = slice(tile * TILE, (tile + 1) * TILE)
        out_ref[span] = jnp.where(
            bounds_ref[span, CROSS : CROSS + 1] > 0.5,
            theirs_ref[span].astype(jnp.float32),
            mine_ref[span].astype(jnp.float32),
        ).astype(jnp.bfloat16)
        swap(tile).wait_send()
    rows.finish()
    outward.finish(viewer(gout_ref, 1 - core))


def attend(queries, pairs, info, prefix, meta, slots, wo):
    heads, count, head = queries.shape
    prompt = (pairs.shape[0] - count, pairs.shape[1])
    tiles = count // TILE
    blocks = 2 * 4
    late = (blocks, wo.shape[0], wo.shape[1] // blocks - EARLY)
    sems = [tiles, tiles, 4, 7, 7] + [Plane.COPIES] * 4 + [2]
    return pl.pallas_call(
        attend_kernel,
        name="attend",
        out_shape=(
            jax.ShapeDtypeStruct((count, heads * head), jnp.bfloat16),
            jax.ShapeDtypeStruct((2, 2, 16, 4) + late[1:], jnp.bfloat16),
        ),
        in_specs=[ANY] * 4 + [SMEM, VMEM],
        out_specs=(VMEM, ANY),
        scratch_shapes=[
            pltpu.VMEM(late, jnp.bfloat16),
            pltpu.VMEM(queries.shape, queries.dtype),
            pltpu.VMEM(pairs.shape, pairs.dtype),
            pltpu.VMEM(info.shape, info.dtype),
            pltpu.VMEM(prefix.shape, prefix.dtype),
            pltpu.VMEM((count, heads * head), jnp.bfloat16),
            pltpu.VMEM((count, heads * head), jnp.bfloat16),
            pltpu.VMEM((32,) + prompt, pairs.dtype),
            pltpu.VMEM((slots * prompt[0], prompt[1]), pairs.dtype),
            pltpu.VMEM(queries.shape, jnp.float32),
            pltpu.VMEM(queries.shape, jnp.float32),
        ]
        + [pltpu.SemaphoreType.DMA((n,)) for n in sems],
        compiler_params=pltpu.CompilerParams(
            collective_id=1, has_side_effects=True, vmem_limit_bytes=60 * 2**20
        ),
    )(queries, pairs, info, prefix, meta, wo)


def return_order(blocks):
    unit, seen, ahead, pace = 1.28, 1.6, 3.0, 8.2
    cost = {"multiply": 1.6, "add": 0.5, "finish": 0.4, "take": 0.3}
    free, summed, order, now = {}, {}, [], 0.0
    waiting = [(max(0.0, pace * p - ahead), 0, ("multiply", p)) for p in range(blocks // 2)]

    def use(link, long):
        free[link] = max(free.get(link, 0.0), now) + long
        return free[link]

    while waiting:
        ready, _, act = waiting.pop(waiting.index(min(waiting)))
        now = max(now, ready) + cost[act[0]]
        order.append(act)
        if act[0] == "multiply":
            both = (2 * act[1], 2 * act[1] + 1)
            for j in both:
                waiting.append((use("y", unit) + seen, 1, ("add", j)))
            for j in both:
                summed[j] = use("y", unit)
        elif act[0] == "add":
            waiting.append((max(use("y", unit), summed[act[1]]) + seen, 2, ("finish", act[1])))
        else:
            j, level = act[1], 0 if act[0] == "finish" else act[2] + 1
            if level < len(LEVELS):
                axis, far = LEVELS[level][0], LEVELS[level][1] == "2"
                links = (axis + "+", axis + "-") if far else (axis + "+-"[j % 2],)
                end = max([use(link, 2 * unit) for link in links]) + (0.5 if far else 0.0)
                waiting.append((end + seen, 3 + level, ("take", j, level)))
    return order


def return_kernel(
    blend_hbm, w0_hbm, w1_hbm, residual_hbm, info_ref, out_ref,
    blend_ref, residual_ref, w0_ref, w1_ref, mask_ref, sums, source, home_sum, home_got, raw, final, held, landed,
    src_send, raw_recv, fin_recv, move_send, move_recv, w_sem,
):
    x, y, z, core = place()
    y_lo, y_hi = lax.rem(y, 2), y // 2
    width = out_ref.shape[1]
    blocks = width // BLOCK
    above, below = step(y, 1), step(y, -1)
    sibling = device_at(x, y, z, 1 - core)
    loads = [
        pltpu.make_async_copy(hbm.at[half], ref.at[half], w_sem.at[n * 2 + half])
        for n, (hbm, ref) in enumerate(((w0_hbm, w0_ref), (w1_hbm, w1_ref)))
        for half in range(2)
    ]
    loads.append(pltpu.make_async_copy(blend_hbm, blend_ref, w_sem.at[4]))
    loads.append(pltpu.make_async_copy(residual_hbm, residual_ref, w_sem.at[5]))
    for load in loads:
        load.start()
    for n in range(mask_ref.shape[0]):
        mask_ref[n] = jnp.broadcast_to(
            info_ref[:, MOVES + n : MOVES + n + 1], mask_ref.shape[1:]
        )
    peers = [device_at(x, at, z, k) for at in (above, below) for k in range(2)] + [sibling]
    peers += [device_at(step(x, s), y, z, core) for s in (1, -1, 2)]
    peers += [device_at(x, y, step(z, s), core) for s in (1, -1, 2)]
    greet(peers)
    home = core == y_lo
    away = jnp.logical_not(home)

    far, up, down = 1 - y_hi, above // 2, below // 2
    quarters = (
        jnp.where(home, far * 2, up * 2),
        jnp.where(home, far * 2 + 1, down * 2 + 1),
        jnp.where(home, y_hi * 2 + 1 - core, up * 2 + 1),
        jnp.where(home, y_hi * 2 + core, down * 2),
    )
    pieces = w0_ref.shape[0]
    half_depth = w0_ref.shape[2] + w1_ref.shape[2]

    for load in loads:
        load.wait()

    def raw_copy(j, slot):
        to = device_at(x, (above, below)[slot], z, core)
        at = slot * blocks + j
        return send(source.at[slot, j], raw.at[slot, j], src_send.at[at], raw_recv.at[at], to)

    def sibling_copy(j):
        at = 2 * blocks + j
        return send(home_sum.at[j], home_got.at[j], src_send.at[at], fin_recv.at[at], sibling)

    def final_copy(j, at):
        slot, k = ((0, 0), (1, 1), (0, 1), (1, 0))[at]
        to = device_at(x, (above, below)[slot], z, k)
        return send(
            source.at[at, j], final.at[slot, j],
            src_send.at[at * blocks + j], fin_recv.at[slot * blocks + j], to,
        )

    def multiply(pair):
        for at in range(4):
            start = pl.multiple_of(quarters[at] * width + pair * 2 * BLOCK, 2 * BLOCK)
            total = None
            for half in range(pieces):
                for n, w_ref in enumerate((w0_ref, w1_ref)):
                    column = half * half_depth + n * w0_ref.shape[2]
                    depth = w_ref.shape[2]
                    term = lax.dot_general(
                        blend_ref[:, column : column + depth], w_ref[half, pl.ds(start, 2 * BLOCK)],
                        (((1,), (1,)), ((), ())), preferred_element_type=jnp.float32,
                    )
                    total = term if total is None else total + term
            sums[at] = total
        lanes = [pl.ds(i * BLOCK, BLOCK) for i in range(2)]

        @pl.when(home)
        def _():
            for i in range(2):
                j = pair * 2 + i
                for slot in range(2):
                    source[slot, j] = sums[slot, :, lanes[i]].astype(jnp.bfloat16)
                    raw_copy(j, slot).start()
            for i in range(2):
                j = pair * 2 + i
                theirs = pl.ds(pl.multiple_of((1 - core) * width + j * BLOCK, BLOCK), BLOCK)
                home_sum[j] = sums[2, :, lanes[i]] + residual_ref[:, theirs].astype(jnp.float32)
                sibling_copy(j).start()
                mine = pl.ds(pl.multiple_of(core * width + j * BLOCK, BLOCK), BLOCK)
                home_got[j] = sums[3, :, lanes[i]] + residual_ref[:, mine].astype(jnp.float32)

        @pl.when(away)
        def _():
            for i in range(2):
                j = pair * 2 + i
                for at in (2, 3):
                    source[at, j] = sums[at, :, lanes[i]].astype(jnp.bfloat16)
                    final_copy(j, at).start()
            for i in range(2):
                j = pair * 2 + i
                for at in range(2):
                    partial[at, j] = sums[at, :, lanes[i]].astype(jnp.bfloat16)

    partial = source

    def add(j):
        @pl.when(away)
        def _():
            for slot in range(2):
                raw_copy(j, slot).wait_recv()
                source[slot, j] = (
                    partial[slot, j].astype(jnp.float32) + raw[slot, j].astype(jnp.float32)
                ).astype(jnp.bfloat16)
                final_copy(j, slot).start()

    def move(j, level):
        by = (1, -1)[j % 2] if LEVELS[level][1] == "1" else 2
        if LEVELS[level][0] == "z":
            to = device_at(x, y, step(z, by), core)
        else:
            to = device_at(step(x, by), y, z, core)
        at = level * blocks + j
        return send(
            held.at[level, j], landed.at[level, j], move_send.at[at], move_recv.at[at], to
        )

    def finish(j):
        for slot in range(2):
            final_copy(j, slot).wait_recv()

        @pl.when(away)
        def _():
            sibling_copy(j).wait_recv()

        total = final[0, j].astype(jnp.float32) + final[1, j].astype(jnp.float32) + home_got[j]
        held[0, j] = total.astype(jnp.bfloat16)
        move(j, 0).start()

    def take(j, level):
        move(j, level).wait_recv()
        chosen = jnp.where(
            mask_ref[(j % 2) * len(LEVELS) + level] > 0.5,
            landed[level, j].astype(jnp.float32),
            held[level, j].astype(jnp.float32),
        ).astype(jnp.bfloat16)
        if level + 1 < len(LEVELS):
            held[level + 1, j] = chosen
            move(j, level + 1).start()
        else:
            out_ref[:, j * BLOCK : (j + 1) * BLOCK] = chosen

    for act, *which in return_order(blocks):
        {"multiply": multiply, "add": add, "finish": finish, "take": take}[act](*which)

    for j in range(blocks):
        for level in range(len(LEVELS)):
            move(j, level).wait_send()

        @pl.when(home)
        def _():
            raw_copy(j, 0).wait_send()
            raw_copy(j, 1).wait_send()
            sibling_copy(j).wait_send()

        @pl.when(away)
        def _():
            for at in range(4):
                final_copy(j, at).wait_send()


def return_rows(blended, w0, w1, residual, info):
    count = blended.shape[0]
    width = residual.shape[1] // 2
    blocks = width // BLOCK
    levels = len(LEVELS)

    def room(n, dtype=jnp.bfloat16):
        return pltpu.VMEM((n, blocks, count, BLOCK), dtype)

    return pl.pallas_call(
        return_kernel,
        name="return_rows",
        out_shape=jax.ShapeDtypeStruct((count, width), jnp.bfloat16),
        in_specs=[ANY] * 4 + [VMEM],
        out_specs=VMEM,
        scratch_shapes=[
            pltpu.VMEM(blended.shape, blended.dtype),
            pltpu.VMEM(residual.shape, residual.dtype),
            pltpu.VMEM(w0.shape, w0.dtype),
            pltpu.VMEM(w1.shape, w1.dtype),
            pltpu.VMEM((2 * levels, count, BLOCK), jnp.float32),
            pltpu.VMEM((4, count, 2 * BLOCK), jnp.float32),
            room(4),
            pltpu.VMEM((blocks, count, BLOCK), jnp.float32),
            pltpu.VMEM((blocks, count, BLOCK), jnp.float32),
            room(2),
            room(2),
            room(levels),
            room(levels),
        ]
        + [pltpu.SemaphoreType.DMA((n * blocks,)) for n in (4, 2, 3, levels, levels)]
        + [pltpu.SemaphoreType.DMA((6,))],
        compiler_params=pltpu.CompilerParams(
            collective_id=2, has_side_effects=True, vmem_limit_bytes=60 * 2**20
        ),
    )(blended, w0, w1, residual, info)


def shards(
    tokens,
    prompt_rows,
    norm_gain,
    w_query,
    w_key,
    w_value,
    w_out,
    q_gain,
    k_gain,
    seq_lengths,
    prompt_group,
    prompt_blocks,
    dest_offset,
):
    width = tokens.shape[1]
    head_size = q_gain.shape[0]
    spread = np.arange(head_size // 2, dtype=np.float32) * np.float32(2.0 / head_size)
    frequency = np.float32(rope_base) ** -spread
    frequency = jnp.asarray(np.tile(frequency.astype(np.float32), 2)[None, :])
    outward = w_out.T
    queries, pairs, residual, prefix, meta, info, gout = project(
        seq_lengths, dest_offset, prompt_group, prompt_blocks, tokens, prompt_rows,
        w_query, w_key, w_value, outward,
        norm_gain[None, :], q_gain[None, :], k_gain[None, :], frequency,
    )
    slots = seq_lengths.shape[0]
    blended, gout_b = attend(queries, pairs, info, prefix, meta, slots, outward)
    features = 4 * width
    return return_rows(
        blended, gout.reshape(2, features, -1), gout_b.reshape(2, features, -1), residual, info
    )


def solution(mesh):
    return jax.shard_map(
        shards,
        mesh=mesh,
        in_specs=(
            P("rep", "tp"),
            P("rep", "tp"),
            P(),
            P(("rep", "tp"), None),
            P(("rep", "tp"), None),
            P(("rep", "tp"), None),
            P(None, ("rep", "tp")),
            P(),
            P(),
            P(),
            P("rep"),
            P("rep"),
            P(),
        ),
        out_specs=P("rep", "tp"),
        check_vma=False,
    )
```

```python
import functools

import jax
import jax.numpy as jnp
import numpy as np
from jax import lax
from jax.experimental import pallas as pl
from jax.experimental.pallas import tpu as pltpu
from jax.sharding import PartitionSpec as P

PBLK = 64
PBLOCKS = 2
MESH = pl.DeviceIdType.MESH
ANY = pl.BlockSpec(memory_space=pl.ANY)
VMEM = pl.BlockSpec(memory_space=pltpu.VMEM)
SMEM = pl.BlockSpec(memory_space=pltpu.SMEM)
OFFSETS = (0, -1, 1, 2)
META = 16
CROSS, START, PROMPT, SLOT, WITHIN, MOVES = 0, 1, 2, 3, 4, 8
EARLY = 256

epsilon = 1e-06
rope_base = 1000000.0


def place():
    rep, tp = lax.axis_index("rep"), lax.axis_index("tp")
    return lax.rem(rep // 4, 4), (tp // 2) * 2 + rep // 16, lax.rem(rep, 4), lax.rem(tp, 2)


def device_at(x, y, z, core):
    return (lax.rem(y, 2) * 16 + x * 4 + z, (y // 2) * 2 + core)


def step(value, by):
    return lax.rem(value + (by + 4), 4)


def greet(peers):
    barrier = pltpu.get_barrier_semaphore()
    for peer in peers:
        pl.semaphore_signal(barrier, inc=1, device_id=peer, device_id_type=MESH)
    pl.semaphore_wait(barrier, len(peers))


def send(source, target, send_sem, recv_sem, device):
    return pltpu.make_async_remote_copy(
        src_ref=source,
        dst_ref=target,
        send_sem=send_sem,
        recv_sem=recv_sem,
        device_id=device,
        device_id_type=MESH,
    )


class Plane:
    COPIES = 72

    def __init__(self, view, send_sems, recv_sems):
        self.view, self.ss, self.rs = view, send_sems, recv_sems
        self.x, self.y, self.z, self.core = place()
        self.started = []

    def block(self, half, first, second, part=None):
        a, b = (first, second) if half == 0 else (second, first)
        return self.view(half, step(self.x, a) * 4 + step(self.z, b), part)

    def toward(self, half, phase, sign):
        if (phase == 0) == (half == 0):
            return device_at(step(self.x, sign), self.y, self.z, self.core)
        return device_at(self.x, self.y, step(self.z, sign), self.core)

    def copy(self, half, number, ref, device):
        at = half * 36 + number
        return send(ref, ref, self.ss.at[at], self.rs.at[at], device)

    def start(self, *args):
        made = self.copy(*args)
        made.start()
        self.started.append(made)

    def sibling(self):
        return device_at(self.x, self.y, self.z, 1 - self.core)

    def share(self, half, o1, o2):
        ref = self.block(half, OFFSETS[o1], OFFSETS[o2])
        self.start(half, 20 + 4 * o1 + o2, ref, self.sibling())

    def spread(self, half, o1):
        ref = self.block(half, OFFSETS[o1], 0)
        self.start(half, 4 + 4 * o1, ref, self.toward(half, 1, 1))
        self.start(half, 5 + 4 * o1, ref, self.toward(half, 1, -1))
        self.share(half, o1, 0)

    def begin(self):
        for half in range(2):
            ref = self.block(half, 0, 0)
            self.start(half, 0, ref, self.toward(half, 0, 1))
            self.start(half, 1, ref, self.toward(half, 0, -1))
        for half in range(2):
            self.spread(half, 0)

    def arrived(self, half, number, ref):
        self.copy(half, number, ref, self.sibling()).wait_recv()

    def first(self):
        for half in range(2):
            self.arrived(half, 0, self.block(half, -1, 0))
            self.start(half, 2, self.block(half, -1, 0, 0), self.toward(half, 0, 1))
            self.arrived(half, 1, self.block(half, 1, 0))
            self.start(half, 3, self.block(half, 1, 0, 1), self.toward(half, 0, -1))
        for half in range(2):
            self.spread(half, 1)
            self.spread(half, 2)

    def opposite(self):
        for half in range(2):
            self.arrived(half, 2, self.block(half, 2, 0, 0))
            self.arrived(half, 3, self.block(half, 2, 0, 1))
            self.spread(half, 3)

    def second(self, o1):
        off, base = OFFSETS[o1], 4 + 4 * o1
        for half in range(2):
            self.arrived(half, base, self.block(half, off, -1))
            self.start(half, base + 2, self.block(half, off, -1, 0), self.toward(half, 1, 1))
            self.arrived(half, base + 1, self.block(half, off, 1))
            self.start(half, base + 3, self.block(half, off, 1, 1), self.toward(half, 1, -1))
            self.share(half, o1, 1)
            self.share(half, o1, 2)

    def second_opposite(self, o1):
        off, base = OFFSETS[o1], 4 + 4 * o1
        for half in range(2):
            self.arrived(half, base + 2, self.block(half, off, 2, 0))
            self.arrived(half, base + 3, self.block(half, off, 2, 1))
            self.share(half, o1, 3)

    def rest(self):
        yield functools.partial(self.second, 0)
        for o1 in range(1, 4):
            yield functools.partial(self.second, o1)
            yield functools.partial(self.second_opposite, o1 - 1)
        yield functools.partial(self.second_opposite, 3)

    def second_all(self):
        for act in self.rest():
            act()

    def finish(self, shared_block):
        for half in range(2):
            for o1 in range(4):
                for o2 in range(4):
                    a, b = (o1, o2) if half == 0 else (o2, o1)
                    where = step(self.x, OFFSETS[a]) * 4 + step(self.z, OFFSETS[b])
                    self.arrived(half, 20 + 4 * o1 + o2, shared_block(half, where))
        for made in self.started:
            made.wait_send()


COLUMN = tuple((dy, dc) for dy in range(4) for dc in range(2) if (dy, dc) != (0, 0))


def column_peers():
    x, y, z, core = place()
    return [device_at(x, step(y, dy), z, core if dc == 0 else 1 - core) for dy, dc in COLUMN]


def plane_peers():
    x, y, z, core = place()
    peers = [device_at(step(x, s), y, z, core) for s in (1, -1)]
    return peers + [device_at(x, y, step(z, s), core) for s in (1, -1)]


class Column:
    def __init__(self, source, land, send_sems, recv_sems, local_sem, which):
        x, y, z, core = place()
        tp = lax.axis_index("tp")
        base = which * len(COLUMN)
        y_lo = lax.rem(y, 2)
        self.local = pltpu.make_async_copy(
            source.at[y * 2 + core], land(core, y_lo, tp), local_sem.at[which]
        )
        self.sent, self.got = [], []
        for n, (dy, dc) in enumerate(COLUMN):
            to_y, from_y = step(y, dy), step(y, -dy)
            peer = core if dc == 0 else 1 - core
            sems = send_sems.at[base + n], recv_sems.at[base + n]
            to = device_at(x, to_y, z, peer)
            self.sent.append(send(source.at[to_y * 2 + peer], land(peer, y_lo, tp), *sems, to))
            ref = land(core, lax.rem(from_y, 2), (from_y // 2) * 2 + peer)
            self.got.append(send(ref, ref, *sems, to))

    def start(self):
        self.local.start()
        for made in self.sent:
            made.start()

    def ready(self):
        self.local.wait()
        for made in self.got:
            made.wait_recv()

    def finish(self):
        for made in self.sent:
            made.wait_send()


def lander(target):
    x, _, z, _ = place()
    return lambda core, y_lo, tp: target.at[core, y_lo, x * 4 + z, tp]


def viewer(target, owner):
    def view(half, where, part=None):
        if part is None:
            return target.at[owner, half, where]
        return target.at[owner, half, where, pl.ds(part * 2, 2)]

    return view


BLOCK = 128
LEVELS = ("z1", "x1", "z2", "x2")


def count_of(condition):
    return jnp.where(condition, 1, 0)


def level_bits(shift, sign):
    odd = (shift & 1) == 1
    far = (shift >= 2) if sign == 1 else ((shift == 1) | (shift == 2))
    return odd, far


def along_z(shift, z):
    return (shift >> 2) + count_of(z < (shift & 3))


def y_shift(shift, x, z):
    need_x = along_z(shift, (z + shift) & 3)
    end_x = (x + need_x) & 3
    return (((need_x >> 2) + count_of(end_x < (need_x & 3))) & 1) == 1


def move_masks(shift, x, z):
    masks = []
    for sign in (1, -1):
        odd_z, far_z = level_bits(shift & 3, sign)
        for level in LEVELS:
            end_z = (z + 2 * count_of(far_z)) & 3 if level in ("z1", "x1") else z
            odd_x, far_x = level_bits(along_z(shift, end_z) & 3, sign)
            masks.append({"z1": odd_z, "x1": odd_x, "z2": far_z, "x2": far_x}[level])
    return masks


def row_info(first, rows, lengths_ref, offsets_ref, prompt_len, x, z):
    shape = (rows, 128)
    row = lax.broadcasted_iota(jnp.int32, shape, 0) + first
    lane = lax.broadcasted_iota(jnp.int32, shape, 1)
    slot, start = jnp.zeros(shape, jnp.int32), jnp.zeros(shape, jnp.int32)
    shift, end = jnp.zeros(shape, jnp.int32) + offsets_ref[0], 0
    for j in range(1, lengths_ref.shape[0]):
        end = end + lengths_ref[j - 1]
        past = row >= end
        slot = slot + count_of(past)
        start = jnp.where(past, end, start)
        shift = jnp.where(past, offsets_ref[j], shift)
    lanes = {
        CROSS: count_of(y_shift(shift, x, z)),
        START: start,
        PROMPT: slot * prompt_len,
        SLOT: slot,
        WITHIN: row - start,
    }
    for n, mask in enumerate(move_masks(shift, x, z)):
        lanes[MOVES + n] = count_of(mask)
    info = jnp.zeros(shape, jnp.int32)
    for at, values in lanes.items():
        info = jnp.where(lane == at, values, info)
    return info.astype(jnp.float32)


def project_kernel(
    lengths_ref, offsets_ref, group_ref, blocks_ref, tokens_ref, prompt_ref,
    wq_ref, wk_ref, wv_ref, wo_ref, gain_ref, q_gain_ref, k_gain_ref, turn_ref,
    q_ref, pairs_ref, residual_ref, prefix_ref, meta_ref, info_ref, gout_ref,
    x_ref, win_ref, wout_ref, rows, theirs, gin, stage, scaled, sums, squares, turn,
    a_send, a_recv, in_send, in_recv, out_send, out_recv, t_send, t_recv, p_send, p_recv, local_sem,
):
    x, y, z, core = place()
    tp = lax.axis_index("tp")
    y_lo, y_hi = lax.rem(y, 2), y // 2
    sibling = device_at(x, y, z, 1 - core)
    above, below = step(y, 1), step(y, -1)
    row_count = residual_ref.shape[0]
    loads, at = [], 0
    for n, ref in enumerate((tokens_ref, prompt_ref)):
        loads.append(
            pltpu.make_async_copy(ref, x_ref.at[pl.ds(at, ref.shape[0])], local_sem.at[3 + n])
        )
        at += ref.shape[0]
    for load in loads:
        load.start()
    slots = group_ref.shape[0]
    lane = lax.broadcasted_iota(jnp.int32, (META, x_ref.shape[1]), 1)
    marks = jnp.zeros(lane.shape, jnp.int32)
    for j in range(slots):
        marks = jnp.where(lane == j, group_ref[j], marks)
        marks = jnp.where(lane == slots + j, blocks_ref[j], marks)
    x_ref[at:] = marks.astype(jnp.float32).astype(jnp.bfloat16)
    blocks, _, block_width = win_ref.shape
    head = q_ref.shape[2]
    wide = block_width - head
    for n in range(blocks):
        win_ref[n, :, :wide] = wq_ref[:, n * wide : (n + 1) * wide].astype(jnp.bfloat16)
        column = n // 2 * head
        narrow_ref = (wk_ref, wv_ref)[n % 2]
        win_ref[n, :, wide:] = narrow_ref[:, column : column + head].astype(jnp.bfloat16)
        wout_ref[n] = wo_ref[:, n * wide : n * wide + EARLY].astype(jnp.bfloat16)
    greet(column_peers() + plane_peers())
    inward_rows = Column(
        win_ref, lambda _, lo, at: stage.at[lo, at], a_send, a_recv, local_sem, 0
    )
    outward_rows = Column(wout_ref, lander(gout_ref), a_send, a_recv, local_sem, 1)
    inward_rows.start()
    outward_rows.start()
    for load in loads:
        load.wait()

    count, width = x_ref.shape
    cut = count // 32 * 16
    parts = (pl.ds(0, cut), pl.ds(cut, count - cut))
    home = core == y_lo
    away = jnp.logical_not(home)

    def quarter(at):
        return pl.ds(pl.multiple_of(at * width, 128), width)

    def own_part(up, part):
        to = device_at(x, above if up else below, z, y_lo)
        at = (0 if up else 4) + core * 2 + part
        ref = rows.at[parts[part], quarter(tp)]
        return send(x_ref.at[parts[part]], ref, t_send.at[(0 if up else 2) + part], t_recv.at[at], to)

    def token_copy(number, ref, device, source=None):
        source = ref if source is None else source
        return send(source, ref, t_send.at[number], t_recv.at[number], device)

    def pass_on(i):
        source = rows.at[pl.ds(0, row_count), quarter(y_hi * 2 + i)]
        target = theirs.at[:, pl.ds(i * width, width)]
        return send(source, target, p_send.at[i], p_recv.at[i], sibling)

    mine = rows.at[:, quarter(tp)]
    keep = pltpu.make_async_copy(x_ref, mine, local_sem.at[2])
    own_parts = [own_part(True, 0), own_part(False, 1), own_part(True, 1), own_part(False, 0)]
    for made in own_parts:
        made.start()

    @pl.when(home)
    def _():
        keep.start()

    @pl.when(away)
    def _():
        token_copy(8, mine, sibling, x_ref).start()

    for tile in range(row_count // 64):
        info_ref[tile * 64 : (tile + 1) * 64] = row_info(
            tile * 64, 64, lengths_ref, offsets_ref, prompt_ref.shape[0], x, z
        )

    def gin_viewer(owner):
        size = stage.shape[1] * stage.shape[2]

        def view(half, where, part=None):
            start = (half * 16 + where) * size
            if part is None:
                return gin.at[owner, pl.ds(pl.multiple_of(start, 16), size)]
            start = start + part * (size // 2)
            return gin.at[owner, pl.ds(pl.multiple_of(start, 16), size // 2)]

        return view

    inward = Plane(gin_viewer(core), in_send, in_recv)
    outward = Plane(viewer(gout_ref, core), out_send, out_recv)
    inward_rows.ready()
    for half in range(2):
        block = stage[half].astype(jnp.float32)
        inward.block(half, 0, 0)[...] = block.reshape(-1, block.shape[-1]).astype(jnp.bfloat16)
    inward.begin()
    inward.first()
    inward.opposite()
    outward_rows.ready()
    outward.begin()
    row_tile = 64
    acts = list(inward.rest())

    def fill_turns(tile):
        lane = lax.broadcasted_iota(jnp.int32, (row_tile, turn.shape[3]), 1)
        sign = jnp.where(lane < turn.shape[3] // 2, -1.0, 1.0)
        span = slice(tile * row_tile, (tile + 1) * row_tile)
        if tile * row_tile < row_count:
            starts = [info_ref[span, WITHIN : WITHIN + 1] + PBLK * (n + 1) for n in range(PBLOCKS)]
        else:
            first = lax.broadcasted_iota(jnp.int32, (row_tile, 1), 0).astype(jnp.float32)
            starts = [first + (tile * row_tile - row_count)]
        for n, start in enumerate(starts):
            angles = start * turn_ref[0:1]
            turn[n, 0, span] = jnp.cos(angles)
            turn[n, 1, span] = jnp.sin(angles) * sign

    fill_turns(0)
    fill_turns(1)
    for act in acts[:3]:
        act()
        fill_turns(acts.index(act) + 2)

    low, high = (below // 2) * 2, (above // 2) * 2

    @pl.when(away)
    def _():
        for k in range(2):
            ref = rows.at[parts[0], quarter(low + k)]
            token_copy(k * 2, ref, sibling).wait_recv()
            token_copy(9 + k, ref, device_at(x, above, z, core)).start()
            ref = rows.at[parts[1], quarter(high + k)]
            token_copy(4 + k * 2 + 1, ref, sibling).wait_recv()
            token_copy(11 + k, ref, device_at(x, below, z, core)).start()

    for n, act in enumerate(acts[3:]):
        act()
        if n < 4:
            fill_turns(n + 5)
    outward.first()
    inward.finish(gin_viewer(1 - core))
    outward.opposite()
    later = list(outward.rest())

    def multiply(i):
        at = quarter(y_hi * 2 + i if i < 2 else (1 - y_hi) * 2 + i - 2)
        gain = gain_ref[:, at]
        for tile in range(scaled.shape[0] // row_tile):
            span = pl.ds(tile * row_tile, row_tile)
            values = rows[span, at].astype(jnp.float32)
            total = jnp.sum(values * values, axis=1, keepdims=True)
            total = jnp.broadcast_to(total, (row_tile, squares.shape[1]))
            squares[span] = total if i == 0 else squares[span] + total
            scaled[span] = (values * gain).astype(jnp.bfloat16)
        for half in range(2):
            term = jnp.dot(scaled[...], gin[half, at], preferred_element_type=jnp.float32)
            sums[half] = term if i == 0 else sums[half] + term

    @pl.when(away)
    def _():
        for k in range(2):
            token_copy(k * 2 + 1, rows.at[parts[1], quarter(low + k)], sibling).wait_recv()
            token_copy(4 + k * 2, rows.at[parts[0], quarter(high + k)], sibling).wait_recv()
        for i in range(2):
            pass_on(i).start()

    @pl.when(home)
    def _():
        keep.wait()
        token_copy(8, rows.at[:, quarter(y_hi * 2 + 1 - core)], sibling).wait_recv()

    for i in range(2):
        multiply(i)
    for act in later[:4]:
        act()

    @pl.when(home)
    def _():
        for i in range(2):
            pass_on(i).wait_recv()
        for i in range(2):
            for tile in range(row_count // row_tile):
                span = pl.ds(tile * row_tile, row_tile)
                lanes = slice(i * width, (i + 1) * width)
                residual_ref[span, lanes] = jnp.where(
                    info_ref[span, CROSS : CROSS + 1] > 0.5,
                    theirs[span, lanes].astype(jnp.float32),
                    rows[span, quarter(y_hi * 2 + i)].astype(jnp.float32),
                ).astype(jnp.bfloat16)

    for k in range(2):

        @pl.when(home)
        def _():
            at = (1 - y_hi) * 2 + k
            for part in range(2):
                token_copy(9 + 2 * part + k, rows.at[parts[part], quarter(at)], sibling).wait_recv()

        multiply(2 + k)

    meta = rows[count - META : count, 0:128].astype(jnp.float32)
    meta_ref[...] = meta.astype(jnp.int32)
    meta = meta[0:1]
    half_heads = q_ref.shape[0] // 2
    for tile in range(scaled.shape[0] // row_tile):
        span = slice(tile * row_tile, (tile + 1) * row_tile)
        scale = lax.rsqrt(squares[span] * (1.0 / (4 * width)) + epsilon)
        if tile * row_tile < row_count:
            lane = lax.broadcasted_iota(jnp.int32, (row_tile, 128), 1).astype(jnp.float32)
            blocks = jnp.sum(
                jnp.where(lane == info_ref[span, SLOT : SLOT + 1] + slots, meta, 0.0),
                axis=1, keepdims=True,
            )
            prefix_ref[span] = jnp.broadcast_to(blocks * PBLK, (row_tile, 128))
            two = jnp.broadcast_to(blocks, (row_tile, head)) > 1.5
            turns = [jnp.where(two, turn[1, n, span], turn[0, n, span]) for n in range(2)]
        else:
            turns = [turn[0, n, span] for n in range(2)]

        def turned(values, gain):
            values = values * scale
            values = values * lax.rsqrt(jnp.mean(values * values, axis=1, keepdims=True) + epsilon)
            values = values * gain
            swapped = jnp.concatenate([values[:, head // 2 :], values[:, : head // 2]], axis=1)
            return (values * turns[0] + swapped * turns[1]).astype(jnp.bfloat16)

        if tile * row_tile < row_count:
            for h in range(2 * half_heads):
                column = h % half_heads * head
                q_ref[h, span] = turned(
                    sums[h // half_heads, span, column : column + head], q_gain_ref[...]
                )
        column = half_heads * head
        pairs_ref[span, :head] = turned(sums[0, span, column : column + head], k_gain_ref[...])
        pairs_ref[span, head:] = (sums[1, span, column : column + head] * scale).astype(jnp.bfloat16)

    for act in later[4:]:
        act()
    outward.finish(viewer(gout_ref, 1 - core))
    inward_rows.finish()
    outward_rows.finish()
    for made in own_parts:
        made.wait_send()

    @pl.when(away)
    def _():
        for k in range(2):
            token_copy(9 + k, rows.at[parts[0], quarter(low + k)], sibling).wait_send()
            token_copy(11 + k, rows.at[parts[1], quarter(high + k)], sibling).wait_send()
            pass_on(k).wait_send()
        token_copy(8, mine, sibling, x_ref).wait_send()


def project(lengths, offsets, group, blocks_of, tokens, prompts, wq, wk, wv, wo, *tables):
    row_count, width = tokens.shape
    used = row_count + prompts.shape[0]
    count = used + META
    depth, head = wq.shape[0], tables[-1].shape[1]
    blocks = 2 * wk.shape[1] // head
    heads = 2 * wq.shape[1] // blocks // head
    block_width = wq.shape[1] // blocks + head
    bf16 = jnp.bfloat16
    planes = [Plane.COPIES] * 4
    return pl.pallas_call(
        project_kernel,
        name="project",
        out_shape=(
            jax.ShapeDtypeStruct((heads, row_count, head), bf16),
            jax.ShapeDtypeStruct((used, 2 * head), bf16),
            jax.ShapeDtypeStruct((row_count, 2 * width), bf16),
            jax.ShapeDtypeStruct((row_count, 128), jnp.float32),
            jax.ShapeDtypeStruct((META, 128), jnp.int32),
            jax.ShapeDtypeStruct((row_count, 128), jnp.float32),
            jax.ShapeDtypeStruct((2, 2, 16, 4, depth, EARLY), bf16),
        ),
        in_specs=[SMEM] * 4 + [ANY] * 2 + [VMEM] * (4 + len(tables)),
        out_specs=(VMEM,) * 6 + (ANY,),
        scratch_shapes=[
            pltpu.VMEM((count, width), bf16),
            pltpu.VMEM((blocks, depth, block_width), bf16),
            pltpu.VMEM((blocks, depth, EARLY), bf16),
            pltpu.VMEM((count, 4 * width), bf16),
            pltpu.VMEM((row_count, 2 * width), bf16),
            pltpu.VMEM((2, 4 * width, block_width), bf16),
            pltpu.VMEM((2, 4, depth, block_width), bf16),
            pltpu.VMEM((used, width), bf16),
            pltpu.VMEM((2, used, block_width), jnp.float32),
            pltpu.VMEM((used, 128), jnp.float32),
            pltpu.VMEM((PBLOCKS, 2, used, head), jnp.float32),
        ]
        + [pltpu.SemaphoreType.DMA((n,)) for n in [14, 14] + planes + [13, 13, 2, 2, 6]],
        compiler_params=pltpu.CompilerParams(
            collective_id=0, has_side_effects=True, vmem_limit_bytes=60 * 2**20
        ),
    )(lengths, offsets, group, blocks_of, tokens, prompts, wq, wk, wv, wo, *tables)


TILE = 64


def attend_kernel(
    q_hbm, pairs_hbm, info_hbm, prefix_hbm, group_ref, wo_ref, out_ref, gout_ref,
    wout_ref, q_ref, pairs_ref, bounds_ref, prefix_ref, mine_ref, theirs_ref,
    prompts, shared, total, sums, x_send, x_recv, load_sem, a_send, a_recv, out_send, out_recv, kv_send, kv_recv, local_sem,
):
    x, y, z, core = place()
    heads, row_count, head = q_ref.shape
    loads = [
        pltpu.make_async_copy(hbm, ref, load_sem.at[n])
        for n, (hbm, ref) in enumerate(
            ((pairs_hbm, pairs_ref), (q_hbm, q_ref), (info_hbm, bounds_ref), (prefix_hbm, prefix_ref))
        )
    ]
    for load in loads:
        load.start()
    own_ref = pairs_ref.at[pl.ds(0, row_count)]
    prompt_ref = pairs_ref.at[pl.ds(row_count, prompts.shape[1])]
    sibling = device_at(x, y, z, 1 - core)
    blocks = wout_ref.shape[0]
    wide = wo_ref.shape[1] // blocks
    for n in range(blocks):
        wout_ref[n] = wo_ref[:, n * wide + EARLY : (n + 1) * wide].astype(jnp.bfloat16)
    greet(column_peers() + plane_peers())
    for load in loads:
        load.wait()
    mine = pltpu.make_async_copy(prompt_ref, prompts.at[core * 16 + x * 4 + z], local_sem.at[1])
    mine.start()
    rows = Column(wout_ref, lander(gout_ref), a_send, a_recv, local_sem, 0)
    rows.start()
    mine.wait()

    def prompt_viewer(owner):
        def view(half, where, part=None):
            span = pl.ds(half * 64, 64) if part is None else pl.ds(half * 64 + part * 32, 32)
            return prompts.at[owner * 16 + where, span]

        return view

    kv = Plane(prompt_viewer(core), kv_send, kv_recv)
    outward = Plane(viewer(gout_ref, core), out_send, out_recv)
    kv.begin()
    scale = head ** (-0.5) * 1.4426950408889634

    def weigh(tile, keys, values, low, high):
        span = pl.ds(tile * TILE, TILE)
        queries = q_ref[:, span].reshape(heads * TILE, head)
        scores = lax.dot_general(
            queries, keys, (((1,), (1,)), ((), ())), preferred_element_type=jnp.float32
        )
        count = keys.shape[0]
        at = lax.broadcasted_iota(jnp.int32, (TILE, count), 1).astype(jnp.float32)
        allowed = (at >= low) & (at < high)
        weights = jnp.where(
            allowed[None], jnp.exp2(scores.reshape(heads, TILE, count) * scale), 0.0
        )
        blend = jnp.dot(
            weights.astype(jnp.bfloat16).reshape(heads * TILE, count), values,
            preferred_element_type=jnp.float32,
        )
        return span, jnp.sum(weights, axis=-1, keepdims=True), blend.reshape(heads, TILE, head)

    def own_tile(tile):
        span = slice(tile * TILE, (tile + 1) * TILE)
        count = min(-(-(tile + 1) * TILE // 128) * 128, row_count)
        low = bounds_ref[span, START : START + 1]
        high = lax.broadcasted_iota(jnp.int32, (TILE, 1), 0).astype(jnp.float32) + (tile * TILE + 1.0)
        span, weight, blend = weigh(tile, own_ref[:count, :head], own_ref[:count, head:], low, high)
        total[:, span] = blend
        sums[:, span] = jnp.broadcast_to(weight, (heads, TILE, head))

    def shared_tile(tile):
        span = slice(tile * TILE, (tile + 1) * TILE)
        low = bounds_ref[span, PROMPT : PROMPT + 1]
        high = low + prefix_ref[span, 0:1]
        span, weight, blend = weigh(tile, shared[:, :head], shared[:, head:], low, high)
        blend = (total[:, span] + blend) / (sums[:, span] + weight)
        for h in range(heads):
            mine_ref[span, h * head : (h + 1) * head] = blend[h].astype(jnp.bfloat16)
        swap(tile).start()

    def swap(tile):
        span = pl.ds(tile * TILE, TILE)
        return send(
            mine_ref.at[span], theirs_ref.at[span], x_send.at[tile], x_recv.at[tile], sibling
        )

    tiles = q_ref.shape[1] // TILE
    acts = list(kv.rest())
    own_tile(0)
    kv.first()
    own_tile(1)
    rows.ready()
    outward.begin()
    kv.opposite()
    own_tile(2)
    acts[0]()
    own_tile(3)
    for act in acts[1:3]:
        act()
    outward.first()
    own_tile(4)
    for act in acts[3:5]:
        act()
    outward.opposite()
    own_tile(5)
    for act in acts[5:]:
        act()
    own_tile(6)
    kv.finish(prompt_viewer(1 - core))
    for j in range(shared.shape[0] // prompts.shape[1]):
        shared[j * prompts.shape[1] : (j + 1) * prompts.shape[1]] = prompts[group_ref[0, j]]
    later = list(outward.rest())
    for tile in range(tiles):
        later[tile]()
        shared_tile(tile)
    for act in later[tiles:]:
        act()
    for tile in range(tiles):
        swap(tile).wait_recv()
        span = slice(tile * TILE, (tile + 1) * TILE)
        out_ref[span] = jnp.where(
            bounds_ref[span, CROSS : CROSS + 1] > 0.5,
            theirs_ref[span].astype(jnp.float32),
            mine_ref[span].astype(jnp.float32),
        ).astype(jnp.bfloat16)
        swap(tile).wait_send()
    rows.finish()
    outward.finish(viewer(gout_ref, 1 - core))


def attend(queries, pairs, info, prefix, meta, slots, wo):
    heads, count, head = queries.shape
    prompt = (pairs.shape[0] - count, pairs.shape[1])
    tiles = count // TILE
    blocks = 2 * 4
    late = (blocks, wo.shape[0], wo.shape[1] // blocks - EARLY)
    sems = [tiles, tiles, 4, 7, 7] + [Plane.COPIES] * 4 + [2]
    return pl.pallas_call(
        attend_kernel,
        name="attend",
        out_shape=(
            jax.ShapeDtypeStruct((count, heads * head), jnp.bfloat16),
            jax.ShapeDtypeStruct((2, 2, 16, 4) + late[1:], jnp.bfloat16),
        ),
        in_specs=[ANY] * 4 + [SMEM, VMEM],
        out_specs=(VMEM, ANY),
        scratch_shapes=[
            pltpu.VMEM(late, jnp.bfloat16),
            pltpu.VMEM(queries.shape, queries.dtype),
            pltpu.VMEM(pairs.shape, pairs.dtype),
            pltpu.VMEM(info.shape, info.dtype),
            pltpu.VMEM(prefix.shape, prefix.dtype),
            pltpu.VMEM((count, heads * head), jnp.bfloat16),
            pltpu.VMEM((count, heads * head), jnp.bfloat16),
            pltpu.VMEM((32,) + prompt, pairs.dtype),
            pltpu.VMEM((slots * prompt[0], prompt[1]), pairs.dtype),
            pltpu.VMEM(queries.shape, jnp.float32),
            pltpu.VMEM(queries.shape, jnp.float32),
        ]
        + [pltpu.SemaphoreType.DMA((n,)) for n in sems],
        compiler_params=pltpu.CompilerParams(
            collective_id=1, has_side_effects=True, vmem_limit_bytes=60 * 2**20
        ),
    )(queries, pairs, info, prefix, meta, wo)


def return_order(blocks):
    unit, seen, ahead, pace = 1.5, 1.6, 3.0, 9.0
    cost = {"multiply": 1.6, "add": 0.5, "finish": 0.4, "take": 0.3}
    free, summed, order, now = {}, {}, [], 0.0
    waiting = [(max(0.0, pace * p - ahead), 0, ("multiply", p)) for p in range(blocks // 2)]

    def use(link, long):
        free[link] = max(free.get(link, 0.0), now) + long
        return free[link]

    while waiting:
        ready, _, act = waiting.pop(waiting.index(min(waiting)))
        now = max(now, ready) + cost[act[0]]
        order.append(act)
        if act[0] == "multiply":
            both = (2 * act[1], 2 * act[1] + 1)
            for j in both:
                waiting.append((use("y", unit) + seen, 1, ("add", j)))
            for j in both:
                summed[j] = use("y", unit)
        elif act[0] == "add":
            waiting.append((max(use("y", unit), summed[act[1]]) + seen, 2, ("finish", act[1])))
        else:
            j, level = act[1], 0 if act[0] == "finish" else act[2] + 1
            if level < len(LEVELS):
                axis, far = LEVELS[level][0], LEVELS[level][1] == "2"
                links = (axis + "+", axis + "-") if far else (axis + "+-"[j % 2],)
                end = max([use(link, 2 * unit) for link in links]) + (0.5 if far else 0.0)
                waiting.append((end + seen, 3 + level, ("take", j, level)))
    return order


def return_kernel(
    blend_hbm, w0_hbm, w1_hbm, residual_hbm, info_ref, out_ref,
    blend_ref, residual_ref, w0_ref, w1_ref, mask_ref, sums, source, home_sum, home_got, raw, final, held, landed,
    src_send, raw_recv, fin_recv, move_send, move_recv, w_sem,
):
    x, y, z, core = place()
    y_lo, y_hi = lax.rem(y, 2), y // 2
    width = out_ref.shape[1]
    blocks = width // BLOCK
    above, below = step(y, 1), step(y, -1)
    sibling = device_at(x, y, z, 1 - core)
    loads = [
        pltpu.make_async_copy(hbm.at[half], ref.at[half], w_sem.at[n * 2 + half])
        for n, (hbm, ref) in enumerate(((w0_hbm, w0_ref), (w1_hbm, w1_ref)))
        for half in range(2)
    ]
    loads.append(pltpu.make_async_copy(blend_hbm, blend_ref, w_sem.at[4]))
    loads.append(pltpu.make_async_copy(residual_hbm, residual_ref, w_sem.at[5]))
    for load in loads:
        load.start()
    for n in range(mask_ref.shape[0]):
        mask_ref[n] = jnp.broadcast_to(
            info_ref[:, MOVES + n : MOVES + n + 1], mask_ref.shape[1:]
        )
    peers = [device_at(x, at, z, k) for at in (above, below) for k in range(2)] + [sibling]
    peers += [device_at(step(x, s), y, z, core) for s in (1, -1, 2)]
    peers += [device_at(x, y, step(z, s), core) for s in (1, -1, 2)]
    greet(peers)
    home = core == y_lo
    away = jnp.logical_not(home)

    far, up, down = 1 - y_hi, above // 2, below // 2
    quarters = (
        jnp.where(home, far * 2, up * 2),
        jnp.where(home, far * 2 + 1, down * 2 + 1),
        jnp.where(home, y_hi * 2 + 1 - core, up * 2 + 1),
        jnp.where(home, y_hi * 2 + core, down * 2),
    )
    pieces = w0_ref.shape[0]
    half_depth = w0_ref.shape[2] + w1_ref.shape[2]

    for load in loads:
        load.wait()

    def raw_copy(j, slot):
        to = device_at(x, (above, below)[slot], z, core)
        at = slot * blocks + j
        return send(source.at[slot, j], raw.at[slot, j], src_send.at[at], raw_recv.at[at], to)

    def sibling_copy(j):
        at = 2 * blocks + j
        return send(home_sum.at[j], home_got.at[j], src_send.at[at], fin_recv.at[at], sibling)

    def final_copy(j, at):
        slot, k = ((0, 0), (1, 1), (0, 1), (1, 0))[at]
        to = device_at(x, (above, below)[slot], z, k)
        return send(
            source.at[at, j], final.at[slot, j],
            src_send.at[at * blocks + j], fin_recv.at[slot * blocks + j], to,
        )

    def multiply(pair):
        for at in range(4):
            start = pl.multiple_of(quarters[at] * width + pair * 2 * BLOCK, 2 * BLOCK)
            total = None
            for half in range(pieces):
                for n, w_ref in enumerate((w0_ref, w1_ref)):
                    column = half * half_depth + n * w0_ref.shape[2]
                    depth = w_ref.shape[2]
                    term = lax.dot_general(
                        blend_ref[:, column : column + depth], w_ref[half, pl.ds(start, 2 * BLOCK)],
                        (((1,), (1,)), ((), ())), preferred_element_type=jnp.float32,
                    )
                    total = term if total is None else total + term
            sums[at] = total
        lanes = [pl.ds(i * BLOCK, BLOCK) for i in range(2)]

        @pl.when(home)
        def _():
            for i in range(2):
                j = pair * 2 + i
                for slot in range(2):
                    source[slot, j] = sums[slot, :, lanes[i]].astype(jnp.bfloat16)
                    raw_copy(j, slot).start()
            for i in range(2):
                j = pair * 2 + i
                theirs = pl.ds(pl.multiple_of((1 - core) * width + j * BLOCK, BLOCK), BLOCK)
                home_sum[j] = sums[2, :, lanes[i]] + residual_ref[:, theirs].astype(jnp.float32)
                sibling_copy(j).start()
                mine = pl.ds(pl.multiple_of(core * width + j * BLOCK, BLOCK), BLOCK)
                home_got[j] = sums[3, :, lanes[i]] + residual_ref[:, mine].astype(jnp.float32)

        @pl.when(away)
        def _():
            for i in range(2):
                j = pair * 2 + i
                for at in (2, 3):
                    source[at, j] = sums[at, :, lanes[i]].astype(jnp.bfloat16)
                    final_copy(j, at).start()
            for i in range(2):
                j = pair * 2 + i
                for at in range(2):
                    partial[at, j] = sums[at, :, lanes[i]].astype(jnp.bfloat16)

    partial = source

    def add(j):
        @pl.when(away)
        def _():
            for slot in range(2):
                raw_copy(j, slot).wait_recv()
                source[slot, j] = (
                    partial[slot, j].astype(jnp.float32) + raw[slot, j].astype(jnp.float32)
                ).astype(jnp.bfloat16)
                final_copy(j, slot).start()

    def move(j, level):
        by = (1, -1)[j % 2] if LEVELS[level][1] == "1" else 2
        if LEVELS[level][0] == "z":
            to = device_at(x, y, step(z, by), core)
        else:
            to = device_at(step(x, by), y, z, core)
        at = level * blocks + j
        return send(
            held.at[level, j], landed.at[level, j], move_send.at[at], move_recv.at[at], to
        )

    def finish(j):
        for slot in range(2):
            final_copy(j, slot).wait_recv()

        @pl.when(away)
        def _():
            sibling_copy(j).wait_recv()

        total = final[0, j].astype(jnp.float32) + final[1, j].astype(jnp.float32) + home_got[j]
        held[0, j] = total.astype(jnp.bfloat16)
        move(j, 0).start()

    def take(j, level):
        move(j, level).wait_recv()
        chosen = jnp.where(
            mask_ref[(j % 2) * len(LEVELS) + level] > 0.5,
            landed[level, j].astype(jnp.float32),
            held[level, j].astype(jnp.float32),
        ).astype(jnp.bfloat16)
        if level + 1 < len(LEVELS):
            held[level + 1, j] = chosen
            move(j, level + 1).start()
        else:
            out_ref[:, j * BLOCK : (j + 1) * BLOCK] = chosen

    for act, *which in return_order(blocks):
        {"multiply": multiply, "add": add, "finish": finish, "take": take}[act](*which)

    for j in range(blocks):
        for level in range(len(LEVELS)):
            move(j, level).wait_send()

        @pl.when(home)
        def _():
            raw_copy(j, 0).wait_send()
            raw_copy(j, 1).wait_send()
            sibling_copy(j).wait_send()

        @pl.when(away)
        def _():
            for at in range(4):
                final_copy(j, at).wait_send()


def return_rows(blended, w0, w1, residual, info):
    count = blended.shape[0]
    width = residual.shape[1] // 2
    blocks = width // BLOCK
    levels = len(LEVELS)

    def room(n, dtype=jnp.bfloat16):
        return pltpu.VMEM((n, blocks, count, BLOCK), dtype)

    return pl.pallas_call(
        return_kernel,
        name="return_rows",
        out_shape=jax.ShapeDtypeStruct((count, width), jnp.bfloat16),
        in_specs=[ANY] * 4 + [VMEM],
        out_specs=VMEM,
        scratch_shapes=[
            pltpu.VMEM(blended.shape, blended.dtype),
            pltpu.VMEM(residual.shape, residual.dtype),
            pltpu.VMEM(w0.shape, w0.dtype),
            pltpu.VMEM(w1.shape, w1.dtype),
            pltpu.VMEM((2 * levels, count, BLOCK), jnp.float32),
            pltpu.VMEM((4, count, 2 * BLOCK), jnp.float32),
            room(4),
            pltpu.VMEM((blocks, count, BLOCK), jnp.float32),
            pltpu.VMEM((blocks, count, BLOCK), jnp.float32),
            room(2),
            room(2),
            room(levels),
            room(levels),
        ]
        + [pltpu.SemaphoreType.DMA((n * blocks,)) for n in (4, 2, 3, levels, levels)]
        + [pltpu.SemaphoreType.DMA((6,))],
        compiler_params=pltpu.CompilerParams(
            collective_id=2, has_side_effects=True, vmem_limit_bytes=60 * 2**20
        ),
    )(blended, w0, w1, residual, info)


def shards(
    tokens,
    prompt_rows,
    norm_gain,
    w_query,
    w_key,
    w_value,
    w_out,
    q_gain,
    k_gain,
    seq_lengths,
    prompt_group,
    prompt_blocks,
    dest_offset,
):
    width = tokens.shape[1]
    head_size = q_gain.shape[0]
    spread = np.arange(head_size // 2, dtype=np.float32) * np.float32(2.0 / head_size)
    frequency = np.float32(rope_base) ** -spread
    frequency = jnp.asarray(np.tile(frequency.astype(np.float32), 2)[None, :])
    outward = w_out.T
    queries, pairs, residual, prefix, meta, info, gout = project(
        seq_lengths, dest_offset, prompt_group, prompt_blocks, tokens, prompt_rows,
        w_query, w_key, w_value, outward,
        norm_gain[None, :], q_gain[None, :], k_gain[None, :], frequency,
    )
    slots = seq_lengths.shape[0]
    blended, gout_b = attend(queries, pairs, info, prefix, meta, slots, outward)
    features = 4 * width
    return return_rows(
        blended, gout.reshape(2, features, -1), gout_b.reshape(2, features, -1), residual, info
    )


def solution(mesh):
    return jax.shard_map(
        shards,
        mesh=mesh,
        in_specs=(
            P("rep", "tp"),
            P("rep", "tp"),
            P(),
            P(("rep", "tp"), None),
            P(("rep", "tp"), None),
            P(("rep", "tp"), None),
            P(None, ("rep", "tp")),
            P(),
            P(),
            P(),
            P("rep"),
            P("rep"),
            P(),
        ),
        out_specs=P("rep", "tp"),
        check_vma=False,
    )
```
